256 devices in a mesh: group: 4 (over x), tile: 32 (over z, y), video: 2 (over core).
Axes of the slice: x: 4, y: 4, z: 8, core: 2. Of those that a mesh axis runs over, the one named last changes fastest.
Arguments:
- features: bfloat16 [64, 8, 16, 24, 384], P(('video', 'tile'), 'group'), parts along dimension 0, may hold values from -6 to 6
- group_slot: int32 [4], replicated, may hold values from 0 to 3, each once
- margins: int32 [32, 4], P('tile'), may hold values from 0 to 4, as said below
- norm_gain: float32 [384], replicated, may hold values from 0.1 to 1.9
- kernel: bfloat16 [3, 3, 3, 384, 384], replicated, may hold values from -0.0625 to 0.0625
- conv_bias: float32 [384], replicated, may hold values from -3 to 3
Outputs:
- decoded: bfloat16 [64, 8, 16, 24, 384], P(('video', 'tile'), 'group'), parts along dimension 0
The draws below stay inside these ranges and needn't reach their ends.
There are 2 independent parts, one for each index of `video`. The reference program is written for one: setup_inputs(seed, part) draws one part's arguments, and reference() takes and returns one part's arrays. A program takes and returns all parts, laid end to end along the dimension named above; an argument that names none is the same for every part. Nothing has to cross between parts.
Inputs may be any that keep to these rules, and one draw needn't show every extreme that they name: group_slot is a permutation of 0 to 3. margins[t] is (left, right, up, down) of tile t; a margin is 0 exactly at the image's border and 1 to 4 elsewhere; the margin a tile has toward a neighbour equals the neighbour's margin back; left and right margins depend only on the tile's column, up and down margins are the same for all columns; some margin equals 4.
All inputs are finite; a program needn't handle non-finite values.
Results may differ from the reference program's by a relative error of at most 0.0043.
Values may be sent and summed in bfloat16 or wider, within the bound.
No kernel may reach another device: no remote copies, remote signals or barrier semaphores. Data moves between devices by JAX's collectives and lax.ppermute only.
A program may use at most 128 MiB of HBM per device.

```python
import jax
import jax.numpy as jnp
from jax import lax

C = 384
F = 2
CH = 16
CW = 24
M = 4
GRID_R = 2
FRAMES = 8
N_GROUP = 4
N_TILE = 32


def draw_margins(key, part):
    key_cols, key_rows, key_pick = jax.random.split(key, 3)
    boundaries = N_TILE // GRID_R - 1
    widths = jax.random.randint(key_cols, (boundaries,), 1, M + 1).astype(jnp.int32)
    picked = jax.random.randint(key_pick, (), 0, boundaries)
    widths = jnp.where(jnp.arange(boundaries) == picked, jnp.int32(M), widths)
    height = jax.random.randint(key_rows, (), 1, M + 1).astype(jnp.int32)
    nothing = jnp.zeros((1,), jnp.int32)
    left_cols = jnp.concatenate([nothing, widths])
    right_cols = jnp.concatenate([widths, nothing])
    tile_rows = jnp.arange(N_TILE) // (N_TILE // GRID_R)
    tile_cols = jnp.arange(N_TILE) % (N_TILE // GRID_R)
    left_side = left_cols[tile_cols]
    right_side = right_cols[tile_cols]
    upper = jnp.where(tile_rows > 0, height, 0)
    lower = jnp.where(tile_rows < GRID_R - 1, height, 0)
    return jnp.stack([left_side, right_side, upper, lower], axis=1).astype(jnp.int32)


def block_scale(key, extent, pieces, low, largest):
    def one(dim, parts):
        heights = jax.random.uniform(jax.random.fold_in(jax.random.fold_in(key, 6), dim), (parts,), jnp.float32, low / len(pieces), largest / len(pieces))
        return jnp.repeat(jnp.exp(heights), extent[dim] // parts).reshape((-1,) + (1,) * (len(extent) - dim - 1))

    loudness = one(*pieces[0])
    for cut in pieces[1:]:
        loudness = loudness * one(*cut)
    return loudness


def noise(key, dims, spread, most, cuts=(), kind=jnp.bfloat16):
    gain = block_scale(key, dims, cuts, -0.22, 0.18) if cuts else 1.0
    result = jax.random.normal(key, dims, jnp.float32) * spread * gain
    return jnp.minimum(jnp.maximum(result, -most), most).astype(kind)


def setup_inputs(seed: int = 0, part: int = 0) -> dict:
    streams_of = jax.random.split(jax.random.key(seed), 7)
    part_keys = jax.random.split(jax.random.fold_in(streams_of[6], part), 7)
    return {
        "features": noise(part_keys[0], (N_TILE, FRAMES, CH, CW, C), 1.0, 6.0, ((0, 32), (1, 4))),
        "group_slot": jax.random.permutation(streams_of[1], N_GROUP).astype(jnp.int32),
        "margins": draw_margins(jax.random.fold_in(streams_of[6], 71), part),
        "norm_gain": jnp.clip(1.0 + 0.18 * jax.random.normal(streams_of[3], (C,), jnp.float32), 0.1, 1.9),
        "kernel": noise(streams_of[4], (3, 3, 3, C, C), (27 * C) ** -0.5, 0.0625),
        "conv_bias": noise(streams_of[5], (C,), 0.5, 3.0, (), jnp.float32),
    }


def activate(values, norm_gain):
    widened = values.astype(jnp.float32)
    inv_norm = lax.rsqrt(lax.optimization_barrier(jnp.mean(widened * widened, axis=-1, keepdims=True)) + 1e-06)
    return jax.nn.silu(widened * inv_norm * norm_gain).astype(jnp.bfloat16)

def convolve(padded, kernel, conv_bias, row_count, col_count):
    frame_count = padded.shape[0] - 2
    channels = padded.shape[-1]
    summed = jnp.zeros((frame_count * row_count * col_count, kernel.shape[-1]), jnp.float32)
    for tap_time in range(3):
        for tap_row in range(3):
            window = padded[tap_time:tap_time + frame_count, tap_row:tap_row + row_count]
            stacked = jnp.concatenate([window[:, :, tap_col:tap_col + col_count] for tap_col in range(3)], axis=-1)
            flattened = stacked.reshape(frame_count * row_count * col_count, 3 * channels)
            summed = summed + jnp.dot(flattened, kernel[tap_time, tap_row].reshape(3 * channels, -1), preferred_element_type=jnp.float32)
    return summed.reshape(frame_count, row_count, col_count, -1) + conv_bias

def window_band(step, core, near, far):
    position = jnp.arange(core + 2 * M, dtype=jnp.int32)
    if step == 1:
        return position < M + near
    if step == -1:
        return position >= M + core - far
    return (position >= M - near) & (position < M + core + far)

def rim_weight(step, core, near, far):
    position = jnp.arange(core, dtype=jnp.int32)
    if step == 1:
        distance = position + 1
        margin = near
    elif step == -1:
        distance = core - position
        margin = far
    else:
        return jnp.ones((core,), jnp.float32)
    margin_f = margin.astype(jnp.float32)
    return jnp.maximum(margin_f + 1.0 - distance.astype(jnp.float32), 0.0) / (margin_f + 1.0)

def panel_source(step, core):
    if step == 1:
        return (M + core, M, 0)
    if step == -1:
        return (0, M, core - M)
    return (M, core, 0)

def blend_add(weighted, weight_sum, panel, step_r, step_c, row_dest, col_dest, reaches):
    core_h = weighted.shape[1]
    core_w = weighted.shape[2]
    row_len = panel.shape[1]
    col_len = panel.shape[2]
    placed = jnp.pad(panel.astype(jnp.float32), ((0, 0), (row_dest, core_h - row_dest - row_len), (col_dest, core_w - col_dest - col_len), (0, 0)))
    weight = rim_weight(step_r, core_h, reaches[2], reaches[3])[:, None] * rim_weight(step_c, core_w, reaches[0], reaches[1])[None, :]
    return (weighted + placed * weight[None, :, :, None], weight_sum + weight)

def reference(features, group_slot, margins, norm_gain, kernel, conv_bias):
    tile_count, frames_all, core_h, core_w, channels = features.shape
    grid_cols = tile_count // GRID_R
    by_slot = jnp.argsort(group_slot).astype(jnp.int32)
    blocks = features.reshape(tile_count, N_GROUP, F, core_h, core_w, channels)[:, by_slot]
    timeline = blocks.reshape(GRID_R, grid_cols, frames_all, core_h, core_w, channels)
    timeline = timeline.transpose(2, 0, 3, 1, 4, 5).reshape(frames_all, GRID_R * core_h, grid_cols * core_w, channels)
    activated = jnp.pad(activate(timeline, norm_gain), ((0, 0), (M, M), (M, M), (0, 0)))
    buffer_h = core_h + 2 * M
    buffer_w = core_w + 2 * M

    def tile_conv(tile_index):
        tile_row = (tile_index // grid_cols).astype(jnp.int32)
        tile_col = (tile_index % grid_cols).astype(jnp.int32)
        reaches = margins[tile_index]
        region = lax.dynamic_slice(activated, (jnp.int32(0), tile_row * core_h, tile_col * core_w, jnp.int32(0)), (frames_all, buffer_h, buffer_w, channels))
        inside = window_band(0, core_h, reaches[2], reaches[3])[:, None] & window_band(0, core_w, reaches[0], reaches[1])[None, :]
        region = jnp.where(inside[None, :, :, None], region, jnp.zeros_like(region))
        padded = jnp.pad(region, ((2, 0), (1, 1), (1, 1), (0, 0)))
        return convolve(padded, kernel, conv_bias, buffer_h, buffer_w).astype(jnp.bfloat16)
    tile_outputs = lax.map(tile_conv, jnp.arange(tile_count, dtype=jnp.int32))

    def tile_blend(tile_index):
        reaches = margins[tile_index]
        weighted = jnp.zeros((frames_all, core_h, core_w, channels), jnp.float32)
        weight_sum = jnp.zeros((core_h, core_w), jnp.float32)
        for step_r in (1, 0, -1):
            for step_c in (1, 0, -1):
                source = jnp.clip(tile_index - (step_r * grid_cols + step_c), 0, tile_count - 1)
                outputs = tile_outputs[source]
                row_first, row_len, row_dest = panel_source(step_r, core_h)
                col_first, col_len, col_dest = panel_source(step_c, core_w)
                panel = outputs[:, row_first:row_first + row_len, col_first:col_first + col_len]
                weighted, weight_sum = blend_add(weighted, weight_sum, panel, step_r, step_c, row_dest, col_dest, reaches)
        return (weighted / weight_sum[None, :, :, None]).astype(jnp.bfloat16)
    blended = lax.map(tile_blend, jnp.arange(tile_count, dtype=jnp.int32))
    blended = blended.reshape(tile_count, N_GROUP, F, core_h, core_w, channels)[:, group_slot]
    return blended.reshape(tile_count, frames_all, core_h, core_w, channels)
```

```python
import functools

import jax
import jax.numpy as jnp
from jax import lax
from jax.experimental import pallas as pl
from jax.experimental.pallas import tpu as pltpu
from jax.sharding import PartitionSpec as P

GRID_R = 2
ROWS, COLS, C = 16, 24, 384
CELLS = ROWS * COLS
PAIR = 2 * COLS
TAPS = 9
DEPTH = TAPS * C


def activated(values, gain):
    inv_norm = lax.rsqrt(jnp.mean(values * values, axis=-1, keepdims=True) + 1e-06)
    scaled = values * inv_norm * gain
    silu = 0.5 * scaled * (1.0 + jnp.tanh(0.5 * scaled))
    return silu.astype(jnp.bfloat16).astype(jnp.float32)


def blend_coef(position, tap, core, near, far):
    source = position + (tap - 1)
    near_f, far_f = near.astype(jnp.float32), far.astype(jnp.float32)
    weight_near = jnp.maximum(near - position, 0).astype(jnp.float32) / (near_f + 1.0)
    weight_far = jnp.maximum(far + 1 - core + position, 0).astype(jnp.float32) / (far_f + 1.0)
    kept = jnp.where(source < near, weight_near, 0.0)
    kept = kept + jnp.where(source >= core - far, weight_far, 0.0)
    kept = kept + jnp.where((source >= -near) & (source < core + far), 1.0, 0.0)
    return kept / (weight_near + 1.0 + weight_far)


def fill_coefs(coefs, margins):
    flat = lax.broadcasted_iota(jnp.int32, (CELLS, 128), 0)
    row = (flat * 2731) >> 16
    col = flat - row * COLS
    by_row = {b: blend_coef(row, b, ROWS, margins[0, 2], margins[0, 3]) for b in (0, 2)}
    by_col = {e: blend_coef(col, e, COLS, margins[0, 0], margins[0, 1]) for e in (0, 2)}
    for b in range(3):
        for e in range(3):
            if b == 1 and e == 1:
                continue
            if b == 1:
                coef = by_col[e]
            elif e == 1:
                coef = by_row[b]
            else:
                coef = by_row[b] * by_col[e]
            coefs[3 * b + e] = coef


def shifted(block, left, right):
    rows = block.shape[0]
    place = lax.broadcasted_iota(jnp.int32, block.shape, 0)
    before = pltpu.roll(block, 1, 0)
    after = pltpu.roll(block, rows - 1, 0)
    for n in range(rows // COLS):
        before = jnp.where(place == n * COLS, left[n], before)
        after = jnp.where(place == n * COLS + COLS - 1, right[n], after)
    return before, block, after


def expand(core, halo, gain, coefs, sides, cells, stacked, top, keep):
    zero = jnp.zeros((COLS, C), jnp.float32)
    for f in range(2):
        left = activated(halo[1, f].astype(jnp.float32), gain)
        right = activated(halo[2, f].astype(jnp.float32), gain)
        if keep is not None:
            left, right = jnp.where(keep, left, 0.0), jnp.where(keep, right, 0.0)
        sides[0, f] = left
        sides[1, f] = right
        rim = activated(halo[0, f].astype(jnp.float32), gain)
        if keep is not None:
            rim = jnp.where(keep, rim, 0.0)
        views = shifted(rim, [left[ROWS : ROWS + 1]], [right[ROWS : ROWS + 1]])
        for e in range(3):
            cells[f, e, 0:COLS] = jnp.where(top, views[e], zero)
            cells[f, e, (ROWS + 1) * COLS : (ROWS + 2) * COLS] = jnp.where(top, zero, views[e])

    for f in range(2):

        def widen(k, _):
            first = pl.multiple_of(k * PAIR, 16)
            block = core[pl.ds(pl.multiple_of(f * CELLS + k * PAIR, 16), PAIR), :]
            block = activated(block.astype(jnp.float32), gain)
            if keep is not None:
                block = jnp.where(keep, block, 0.0)
            views = shifted(
                block,
                [sides[0, f, pl.ds(2 * k + n, 1), :] for n in range(2)],
                [sides[1, f, pl.ds(2 * k + n, 1), :] for n in range(2)],
            )
            for e in range(3):
                cells[f, e, pl.ds(pl.multiple_of(first + COLS, 8), PAIR), :] = views[e]
            return 0

        lax.fori_loop(0, ROWS // 2, widen, 0)

    for f in range(2):

        def stack(k, _):
            first = pl.multiple_of(k * PAIR, 16)
            for b in range(3):
                for e in range(3):
                    block = cells[f, e, pl.ds(pl.multiple_of(first + b * COLS, 8), PAIR), :]
                    if b != 1 or e != 1:
                        coef = coefs[3 * b + e, pl.ds(first, PAIR), :]
                        block = block * jnp.concatenate([coef] * (C // 128), axis=1)
                    lanes = slice((3 * b + e) * C, (3 * b + e + 1) * C)
                    stacked[f, pl.ds(first, PAIR), lanes] = block.astype(jnp.bfloat16)
            return 0

        lax.fori_loop(0, ROWS // 2, stack, 0)


def fetch(weights, taps, sems, first, second):
    copies = [
        pltpu.make_async_copy(weights.at[a], taps.at[:, pl.ds(n * C, C)], sems.at[n])
        for n, a in enumerate((first, second))
    ]
    for copy in copies:
        copy.start()
    return copies


def dot(a, b):
    return jnp.dot(a, b, preferred_element_type=jnp.float32)


def own_kernel(margins, where, core, halo, gain, weights, out, taps, coefs, sides, cells, stacked, sems):
    copies = fetch(weights, taps, sems, 2, 1)
    fill_coefs(coefs, margins)
    expand(core, halo, gain[...], coefs, sides, cells, stacked, where[0] == 1, None)
    for copy in copies:
        copy.wait()
    out[0] = dot(stacked[0], taps[:, :C])
    out[1] = dot(stacked[0], taps[:, C:]) + dot(stacked[1], taps[:, :C])


def previous_kernel(
    margins, where, core, halo, gain, weights, own, bias, out, taps, coefs, sides, cells, stacked, sems
):
    copies = fetch(weights, taps, sems, 1, 0)
    fill_coefs(coefs, margins)
    expand(core, halo, gain[...], coefs, sides, cells, stacked, where[0] == 1, where[1] > 0)
    for copy in copies:
        copy.wait()
    first = own[0] + bias[...] + dot(stacked[1], taps[:, :C]) + dot(stacked[0], taps[:, C:])
    out[0:CELLS] = first.astype(jnp.bfloat16)
    second = own[1] + bias[...] + dot(stacked[1], taps[:, C:])
    out[CELLS : 2 * CELLS] = second.astype(jnp.bfloat16)


def call(kernel, inputs, out_shape):
    smem, vmem, hbm = (
        pl.BlockSpec(memory_space=pltpu.SMEM),
        pl.BlockSpec(memory_space=pltpu.VMEM),
        pl.BlockSpec(memory_space=pl.ANY),
    )
    specs = [smem, smem, vmem, vmem, vmem, hbm] + [vmem] * (len(inputs) - 6)
    return pl.pallas_call(
        kernel,
        in_specs=specs,
        out_specs=vmem,
        out_shape=out_shape,
        scratch_shapes=[
            pltpu.VMEM((DEPTH, 2 * C), jnp.bfloat16),
            pltpu.VMEM((TAPS, CELLS, 128), jnp.float32),
            pltpu.VMEM((2, 2, COLS, C), jnp.float32),
            pltpu.VMEM((2, 3, (ROWS + 2) * COLS, C), jnp.float32),
            pltpu.VMEM((2, CELLS, DEPTH), jnp.bfloat16),
            pltpu.SemaphoreType.DMA((2,)),
        ],
        compiler_params=pltpu.CompilerParams(vmem_limit_bytes=44 * 2**20),
        cost_estimate=pl.CostEstimate(
            flops=2 * 3 * CELLS * DEPTH * C, bytes_accessed=8 * 2**20, transcendentals=2 * CELLS * C
        ),
    )(*inputs)


def cyclic_order(index):
    place = index // 2 + 1
    others = [p for p in (1, 2, 3) if p != place]
    if index % 2:
        others = others[::-1]
    places = [0, place] + others
    return sorted(range(4), key=lambda d: places[d])


def local(features, group_slot, margins, norm_gain, kernel, conv_bias):
    tiles = lax.axis_size("tile")
    across = tiles // GRID_R
    tile = lax.axis_index("tile")
    tile_row = tile // across
    slot = group_slot[lax.axis_index("group")]
    where = jnp.stack([tile_row, slot]).astype(jnp.int32)
    weights = kernel.reshape(3, DEPTH, C)
    gain = norm_gain.reshape(1, C)
    bias = conv_bias.reshape(1, C)
    core = features.reshape(2 * CELLS, C)

    def routed(order):
        route = [(order[n], order[(n + 1) % 4]) for n in range(4)]

        def branch(features, where, margins, gain, weights):
            own = features[0]
            previous = lax.ppermute(features, "group", route)
            edge = lax.dynamic_index_in_dim(
                own, jnp.where(where[0] == 1, 0, ROWS - 1), axis=1, keepdims=False
            )
            rim = lax.ppermute(edge, "tile", [(t, (t + across) % tiles) for t in range(tiles)])
            columns = [
                jnp.pad(
                    jnp.concatenate([own[:, :, at], rim[:, at : at + 1]], axis=1),
                    ((0, 0), (0, COLS - ROWS - 1), (0, 0)),
                )
                for at in (COLS - 1, 0)
            ]
            inner = [t for t in range(tiles) if t % across != across - 1]
            left = lax.ppermute(columns[0], "tile", [(t, t + 1) for t in inner])
            right = lax.ppermute(columns[1], "tile", [(t + 1, t) for t in inner])
            halo = jnp.stack([rim, left, right])
            halo_previous = lax.ppermute(halo, "group", route)
            partial = call(
                own_kernel,
                (margins, where, own.reshape(2 * CELLS, C), halo, gain, weights),
                jax.ShapeDtypeStruct((2, CELLS, C), jnp.float32),
            )
            return previous, halo_previous, partial

        return branch

    away = (group_slot[1:] - group_slot[0]) % 4
    index = (away[0] - 1) * 2 + (away[1] > away[2]).astype(jnp.int32)
    previous, halo_previous, partial = lax.switch(
        index,
        [routed(cyclic_order(n)) for n in range(6)],
        features,
        where,
        margins,
        gain,
        weights,
    )
    decoded = call(
        previous_kernel,
        (margins, where, previous.reshape(2 * CELLS, C), halo_previous, gain, weights, partial, bias),
        jax.ShapeDtypeStruct((2 * CELLS, C), jnp.bfloat16),
    )
    return decoded.reshape(1, 2, ROWS, COLS, C)


def solution(mesh):
    return jax.shard_map(
        local,
        mesh=mesh,
        in_specs=(
            P(("video", "tile"), "group", None, None, None),
            P(),
            P("tile", None),
            P(),
            P(),
            P(),
        ),
        out_specs=P(("video", "tile"), "group", None, None, None),
        check_vma=False,
    )
```

```python
import jax
import jax.numpy as jnp
from jax import lax
from jax.experimental import pallas as pl
from jax.experimental.pallas import tpu as pltpu
from jax.sharding import PartitionSpec as P

GRID_R = 2
ROWS, COLS, C = 16, 24, 384
CELLS = ROWS * COLS
PAIR = 2 * COLS
DEPTH = 9 * C


def activated(values, half_gain):
    inv_norm = lax.rsqrt(jnp.mean(values * values, axis=-1, keepdims=True) + 1e-06)
    half = values * inv_norm * half_gain
    silu = half + half * jnp.tanh(half)
    return silu.astype(jnp.bfloat16).astype(jnp.float32)


def blend_coef(position, tap, core, near, far):
    source = position + (tap - 1)
    near_f, far_f = near.astype(jnp.float32), far.astype(jnp.float32)
    weight_near = jnp.maximum(near - position, 0).astype(jnp.float32) / (near_f + 1.0)
    weight_far = jnp.maximum(far + 1 - core + position, 0).astype(jnp.float32) / (far_f + 1.0)
    kept = jnp.where(source < near, weight_near, 0.0)
    kept = kept + jnp.where(source >= core - far, weight_far, 0.0)
    kept = kept + jnp.where((source >= -near) & (source < core + far), 1.0, 0.0)
    return kept / (weight_near + 1.0 + weight_far)


def shifted(block, left, right, coef_first, coef_last):
    size = block.shape[0]
    place = lax.broadcasted_iota(jnp.int32, (8, C), 0)
    before = pltpu.roll(block, 1, 0)
    after = pltpu.roll(block, size - 1, 0)
    before_parts, after_parts = [], []
    for n in range(size // COLS):
        first, middle, last = (slice(n * COLS + at, n * COLS + at + 8) for at in (0, 8, 16))
        before_parts += [
            jnp.where(place == 0, left[n], before[first]),
            before[middle],
            before[last] * coef_first,
        ]
        after_parts += [
            after[first] * coef_last,
            after[middle],
            jnp.where(place == 7, right[n], after[last]),
        ]
    return jnp.concatenate(before_parts, axis=0), block, jnp.concatenate(after_parts, axis=0)


def expand(margins, core, halo, gain, row_coefs, sides, spare, stacked, top, keep):
    place = lax.broadcasted_iota(jnp.int32, (8, C), 0)
    coef_first = blend_coef(place + (COLS - 8), 0, COLS, margins[0, 0], margins[0, 1])
    coef_last = blend_coef(place, 2, COLS, margins[0, 0], margins[0, 1])
    row = lax.broadcasted_iota(jnp.int32, (ROWS, C), 0)
    for n, b in enumerate((0, 2)):
        row_coefs[n] = blend_coef(row, b, ROWS, margins[0, 2], margins[0, 3])
    half_gain = 0.5 * gain
    if keep is not None:
        half_gain = jnp.where(keep, half_gain, 0.0)

    def frame(f, _):
        left = activated(halo[1, f].astype(jnp.float32), half_gain)
        right = activated(halo[2, f].astype(jnp.float32), half_gain)
        sides[0] = left
        sides[1] = right
        rim = activated(halo[0, f].astype(jnp.float32), half_gain)
        rims = shifted(
            rim, [left[ROWS : ROWS + 1]], [right[ROWS : ROWS + 1]], coef_first, coef_last
        )
        for e in range(3):
            spare[0, e] = jnp.where(top, rims[e], 0.0)
            spare[1, e] = jnp.where(top, 0.0, rims[e])

        def lanes(b, e):
            return slice((3 * b + e) * C, (3 * b + e + 1) * C)

        def two_rows(k, scale_above, scale_below, above):
            rows = pl.ds(pl.multiple_of(k * PAIR, 16), PAIR)
            block = core[pl.ds(pl.multiple_of(f * CELLS + k * PAIR, 16), PAIR), :]
            block = activated(block.astype(jnp.float32), half_gain)
            views = shifted(
                block,
                [sides[0, pl.ds(2 * k + n, 1), :] for n in range(2)],
                [sides[1, pl.ds(2 * k + n, 1), :] for n in range(2)],
                coef_first,
                coef_last,
            )
            for e in range(3):
                stacked[f, rows, lanes(1, e)] = views[e].astype(jnp.bfloat16)
                pieces = [spare[0, e], views[e][:COLS]]
                spare[0, e] = views[e][COLS:]

                def put(to, b, scale, first):
                    values = pieces
                    if scale:
                        values = [
                            p * row_coefs[b // 2, pl.ds(first + n, 1), :]
                            for n, p in enumerate(values)
                        ]
                    values = jnp.concatenate(values, axis=0).astype(jnp.bfloat16)
                    stacked[f, pl.ds(pl.multiple_of(to * PAIR, 16), PAIR), lanes(b, e)] = values

                put(k, 0, scale_above, 2 * k)
                if above:
                    put(k - 1, 2, scale_below, 2 * k - 2)

        def loop(first, last, scale_above, scale_below):
            def step(k, _):
                two_rows(k, scale_above, scale_below, True)
                return 0

            lax.fori_loop(first, last, step, 0)

        two_rows(0, False, False, False)
        loop(1, 3, False, True)
        loop(3, 6, False, False)
        loop(6, 8, True, False)
        for e in range(3):
            values = jnp.concatenate([spare[0, e], spare[1, e]], axis=0).astype(jnp.bfloat16)
            stacked[f, (ROWS - 2) * COLS : ROWS * COLS, lanes(2, e)] = values
        return 0

    lax.fori_loop(0, 2, frame, 0)


def fetch(weights, taps, sems, first, second):
    copies = [
        pltpu.make_async_copy(weights.at[a], taps.at[:, pl.ds(n * C, C)], sems.at[n])
        for n, a in enumerate((first, second))
    ]
    for copy in copies:
        copy.start()
    return copies


def dot(a, b):
    return jnp.dot(a, b, preferred_element_type=jnp.float32)


def own_kernel(
    margins, tile_row, core, halo, gain, weights, out, taps, row_coefs, sides, spare, stacked, sems
):
    copies = fetch(weights, taps, sems, 2, 1)
    gain = gain[...].reshape(1, C)
    expand(margins, core, halo, gain, row_coefs, sides, spare, stacked, tile_row[0] == 1, None)
    for copy in copies:
        copy.wait()

    def part(n, _):
        rows = pl.ds(pl.multiple_of(n * 128, 16), 128)
        both = dot(stacked[0, rows, :], taps[...])
        out[0, rows, :] = both[:, :C]
        out[1, rows, :] = both[:, C:] + dot(stacked[1, rows, :], taps[:, :C])
        return 0

    lax.fori_loop(0, CELLS // 128, part, 0)


def previous_kernel(
    margins,
    tile_row,
    core,
    halo,
    gain,
    weights,
    own,
    bias,
    slot,
    out,
    taps,
    row_coefs,
    sides,
    spare,
    stacked,
    sems,
):
    copies = fetch(weights, taps, sems, 1, 0)
    gain = gain[...].reshape(1, C)
    bias = bias[...].reshape(1, C)
    expand(
        margins, core, halo, gain, row_coefs, sides, spare, stacked, tile_row[0] == 1, slot[0] > 0
    )
    for copy in copies:
        copy.wait()
    both = dot(stacked[1], taps[...])
    first = own[0] + bias + both[:, :C] + dot(stacked[0], taps[:, C:])
    out[0:CELLS] = first.astype(jnp.bfloat16)
    out[CELLS : 2 * CELLS] = (own[1] + bias + both[:, C:]).astype(jnp.bfloat16)


SMEM, VMEM, HBM = (pl.BlockSpec(memory_space=m) for m in (pltpu.SMEM, pltpu.VMEM, pl.ANY))


def call(kernel, inputs, specs, out_shape):
    return pl.pallas_call(
        kernel,
        in_specs=specs,
        out_specs=VMEM,
        out_shape=out_shape,
        scratch_shapes=[
            pltpu.VMEM((DEPTH, 2 * C), jnp.bfloat16),
            pltpu.VMEM((2, ROWS, C), jnp.float32),
            pltpu.VMEM((2, COLS, C), jnp.float32),
            pltpu.VMEM((2, 3, COLS, C), jnp.float32),
            pltpu.VMEM((2, CELLS, DEPTH), jnp.bfloat16),
            pltpu.SemaphoreType.DMA((2,)),
        ],
        compiler_params=pltpu.CompilerParams(vmem_limit_bytes=40 * 2**20),
        cost_estimate=pl.CostEstimate(
            flops=2 * 3 * CELLS * DEPTH * C, bytes_accessed=8 * 2**20, transcendentals=2 * CELLS * C
        ),
    )(*inputs)


def prepare_kernel(group_slot, tile_row, core, index, rim, columns):
    away = [(group_slot[d] - group_slot[0] + 4) % 4 for d in (1, 2, 3)]
    index[0] = (away[0] - 1) * 2 + jnp.where(away[1] > away[2], 1, 0)
    top = tile_row[0] == 1
    for f in range(2):
        blocks = [
            core[f * CELLS + k * PAIR : f * CELLS + (k + 1) * PAIR].astype(jnp.float32)
            for k in range(ROWS // 2)
        ]
        rim[f] = jnp.where(top, blocks[0][:COLS], blocks[-1][COLS:]).astype(jnp.bfloat16)
        for side, at in enumerate((0, COLS - 1)):
            cells = [block[at + n : at + n + 1] for block in blocks for n in (0, COLS)]
            columns[side, f] = jnp.concatenate(cells, axis=0).astype(jnp.bfloat16)


def prepare(group_slot, tile_row, core):
    return pl.pallas_call(
        prepare_kernel,
        in_specs=[SMEM, SMEM, VMEM],
        out_specs=[SMEM, VMEM, VMEM],
        out_shape=[
            jax.ShapeDtypeStruct((1,), jnp.int32),
            jax.ShapeDtypeStruct((2, COLS, C), jnp.bfloat16),
            jax.ShapeDtypeStruct((2, 2, ROWS, C), jnp.bfloat16),
        ],
    )(group_slot, tile_row, core)


def cyclic_order(index):
    place = index // 2 + 1
    others = [p for p in (1, 2, 3) if p != place]
    if index % 2:
        others = others[::-1]
    places = [0, place] + others
    return sorted(range(4), key=lambda d: places[d])


def local(features, group_slot, margins, norm_gain, kernel, conv_bias):
    tiles = lax.axis_size("tile")
    across = tiles // GRID_R
    tile_row = (lax.axis_index("tile") // across).astype(jnp.int32).reshape(1)
    slot = group_slot[lax.axis_index("group")].reshape(1)
    weights = kernel.reshape(3, DEPTH, C)
    core = features.reshape(2 * CELLS, C)
    index, edge, edge_columns = prepare(group_slot, tile_row, core)

    def routed(order):
        route = [(order[n], order[(n + 1) % 4]) for n in range(4)]

        def branch(features, edge, edge_columns, tile_row, margins, gain, weights):
            previous = lax.ppermute(features, "group", route)
            rim = lax.ppermute(edge, "tile", [(t, (t + across) % tiles) for t in range(tiles)])
            spare = jnp.zeros((2, COLS - ROWS - 1, C), jnp.bfloat16)
            first, last = (
                jnp.concatenate([edge_columns[side], rim[:, at : at + 1], spare], axis=1)
                for side, at in ((0, 0), (1, COLS - 1))
            )
            inner = [t for t in range(tiles) if t % across != across - 1]
            left = lax.ppermute(last, "tile", [(t, t + 1) for t in inner])
            right = lax.ppermute(first, "tile", [(t + 1, t) for t in inner])
            halo = jnp.stack([rim, left, right])
            halo_previous = lax.ppermute(halo, "group", route)
            partial = call(
                own_kernel,
                (margins, tile_row, features.reshape(2 * CELLS, C), halo, gain, weights),
                [SMEM, SMEM, VMEM, VMEM, VMEM, HBM],
                jax.ShapeDtypeStruct((2, CELLS, C), jnp.float32),
            )
            return previous, halo_previous, partial

        return branch

    previous, halo_previous, partial = lax.switch(
        index[0],
        [routed(cyclic_order(n)) for n in range(6)],
        features,
        edge,
        edge_columns,
        tile_row,
        margins,
        norm_gain,
        weights,
    )
    decoded = call(
        previous_kernel,
        (
            margins,
            tile_row,
            previous.reshape(2 * CELLS, C),
            halo_previous,
            norm_gain,
            weights,
            partial,
            conv_bias,
            slot,
        ),
        [SMEM, SMEM, VMEM, VMEM, VMEM, HBM, VMEM, VMEM, SMEM],
        jax.ShapeDtypeStruct((2 * CELLS, C), jnp.bfloat16),
    )
    return decoded.reshape(1, 2, ROWS, COLS, C)


def solution(mesh):
    return jax.shard_map(
        local,
        mesh=mesh,
        in_specs=(
            P(("video", "tile"), "group", None, None, None),
            P(),
            P("tile", None),
            P(),
            P(),
            P(),
        ),
        out_specs=P(("video", "tile"), "group", None, None, None),
        check_vma=False,
    )
```

```python
import jax
import jax.numpy as jnp
from jax import lax
from jax.experimental import pallas as pl
from jax.experimental.pallas import tpu as pltpu
from jax.sharding import PartitionSpec as P

GRID_R = 2
ROWS, COLS, C = 16, 24, 384
CELLS = ROWS * COLS
PAIR = 2 * COLS
DEPTH = 9 * C


def activated(values, half_gain):
    inv_norm = lax.rsqrt(jnp.mean(values * values, axis=-1, keepdims=True) + 1e-06)
    half = values * inv_norm * half_gain
    silu = half + half * jnp.tanh(half)
    return silu.astype(jnp.bfloat16).astype(jnp.float32)


def blend_coef(position, tap, core, near, far):
    source = position + (tap - 1)
    near_f, far_f = near.astype(jnp.float32), far.astype(jnp.float32)
    weight_near = jnp.maximum(near - position, 0).astype(jnp.float32) / (near_f + 1.0)
    weight_far = jnp.maximum(far + 1 - core + position, 0).astype(jnp.float32) / (far_f + 1.0)
    kept = jnp.where(source < near, weight_near, 0.0)
    kept = kept + jnp.where(source >= core - far, weight_far, 0.0)
    kept = kept + jnp.where((source >= -near) & (source < core + far), 1.0, 0.0)
    return kept / (weight_near + 1.0 + weight_far)


def shifted(block, left, right, coef_first, coef_last):
    size = block.shape[0]
    place = lax.broadcasted_iota(jnp.int32, (8, C), 0)
    before = pltpu.roll(block, 1, 0)
    after = pltpu.roll(block, size - 1, 0)
    before_parts, after_parts = [], []
    for n in range(size // COLS):
        first, middle, last = (slice(n * COLS + at, n * COLS + at + 8) for at in (0, 8, 16))
        before_parts += [
            jnp.where(place == 0, left[n], before[first]),
            before[middle],
            before[last] * coef_first,
        ]
        after_parts += [
            after[first] * coef_last,
            after[middle],
            jnp.where(place == 7, right[n], after[last]),
        ]
    return jnp.concatenate(before_parts, axis=0), block, jnp.concatenate(after_parts, axis=0)


def expand(margins, core, gain, row_coefs, spare, stacked, columns):
    fill_row_coefs(margins, row_coefs)
    coef_first, coef_last = column_coefs(margins)
    half_gain = 0.5 * gain
    zeros = [jnp.zeros((1, C), jnp.float32)] * 4
    spare[...] = jnp.zeros_like(spare)

    def lanes(b, e):
        return slice((3 * b + e) * C, (3 * b + e + 1) * C)

    def put(f, k, b, e, values, scale):
        if scale:
            values = [
                p * row_coefs[b // 2, pl.ds(2 * k + n, 1), :] for n, p in enumerate(values)
            ]
        values = jnp.concatenate(values, axis=0).astype(jnp.bfloat16)
        stacked[f, pl.ds(pl.multiple_of(k * PAIR, 16), PAIR), lanes(b, e)] = values

    def two_rows(k, scale_above, scale_below, above):
        blocks = [
            core[pl.ds(pl.multiple_of(f * CELLS + k * PAIR, 16), PAIR), :].astype(jnp.float32)
            for f in range(2)
        ]
        if columns is not None:
            for f in range(2):
                for n in range(2):
                    first, last = n * COLS, n * COLS + COLS - 1
                    columns[0, f, pl.ds(2 * k + n, 1), :] = blocks[f][first : first + 1]
                    columns[1, f, pl.ds(2 * k + n, 1), :] = blocks[f][last : last + 1]
        block = activated(jnp.concatenate(blocks, axis=0), half_gain)
        views = shifted(block, zeros, zeros, coef_first, coef_last)
        for f in range(2):
            for e in range(3):
                rows = [views[e][(2 * f + n) * COLS : (2 * f + n + 1) * COLS] for n in range(2)]
                put(f, k, 1, e, rows, False)
                odd = [spare[f, e], rows[0]]
                spare[f, e] = rows[1]
                put(f, k, 0, e, odd, scale_above)
                if above:
                    put(f, k - 1, 2, e, odd, scale_below)

    def loop(first, last, scale_above, scale_below):
        def step(k, _):
            two_rows(k, scale_above, scale_below, True)
            return 0

        lax.fori_loop(first, last, step, 0)

    two_rows(0, False, False, False)
    loop(1, 3, False, True)
    loop(3, 6, False, False)
    loop(6, 8, True, False)
    for f in range(2):
        for e in range(3):
            put(f, ROWS // 2 - 1, 2, e, [spare[f, e], jnp.zeros((COLS, C), jnp.float32)], False)


def fill_row_coefs(margins, row_coefs):
    row = lax.broadcasted_iota(jnp.int32, (ROWS, C), 0)
    for n, b in enumerate((0, 2)):
        row_coefs[n] = blend_coef(row, b, ROWS, margins[0, 2], margins[0, 3])


def column_coefs(margins):
    place = lax.broadcasted_iota(jnp.int32, (8, C), 0)
    coef_first = blend_coef(place + (COLS - 8), 0, COLS, margins[0, 0], margins[0, 1])
    coef_last = blend_coef(place, 2, COLS, margins[0, 0], margins[0, 1])
    return coef_first, coef_last


def dot(a, b):
    return jnp.dot(a, b, preferred_element_type=jnp.float32)


def weights_of(weights, times):
    return jnp.concatenate([weights[a] for a in times], axis=1)


def expand_kernel(
    margins, core, gain, weights, stacked, columns, taps, row_coefs, spare, cells, sems
):
    copies = [
        pltpu.make_async_copy(weights.at[2 - n], taps.at[:, pl.ds(n * C, C)], sems.at[n])
        for n in range(3)
    ]
    for copy in copies:
        copy.start()
    expand(margins, core, gain[...].reshape(1, C), row_coefs, spare, stacked, cells)
    columns[...] = cells[...].astype(jnp.bfloat16)
    for copy in copies:
        copy.wait()


def own_kernel(stacked, taps, own):
    def part(n, _):
        rows = pl.ds(pl.multiple_of(n * 128, 16), 128)
        both = dot(stacked[0, rows, :], taps[:, : 2 * C])
        own[0, rows, :] = both[:, :C]
        own[1, rows, :] = both[:, C:] + dot(stacked[1, rows, :], taps[:, :C])
        return 0

    lax.fori_loop(0, CELLS // 128, part, 0)


def previous_kernel(
    margins, group_slot, group, core, gain, taps, own, bias, sums, row_coefs, spare, stacked
):
    bias = bias[...].reshape(1, C)
    gain = jnp.where(group_slot[group[0]] > 0, gain[...].reshape(1, C), 0.0)
    expand(margins, core, gain, row_coefs, spare, stacked, None)

    def part(n, _):
        rows = pl.ds(pl.multiple_of(n * 128, 16), 128)
        both = dot(stacked[1, rows, :], taps[:, C:])
        last = dot(stacked[0, rows, :], taps[:, 2 * C :])
        sums[0, rows, :] = own[0, rows, :] + bias + both[:, :C] + last
        sums[1, rows, :] = own[1, rows, :] + bias + both[:, C:]
        return 0

    lax.fori_loop(0, CELLS // 128, part, 0)


def join_kernel(
    margins, tile_row, group_slot, group, halo, halo_previous, gain, taps, sums, out, row_coefs, sides
):
    fill_row_coefs(margins, row_coefs)
    coef_first, coef_last = column_coefs(margins)
    half_gain = 0.5 * gain[...].reshape(1, C)
    half_previous = jnp.where(group_slot[group[0]] > 0, half_gain, 0.0)
    top = tile_row[0] == 1

    def frame(n, part):
        source, f, scale = (
            (halo_previous, n, half_previous) if n < 2 else (halo, n - 2, half_gain)
        )
        return activated(source[part, f].astype(jnp.float32), scale)

    rims, columns = [], ([], [])
    none = jnp.zeros((1, C), jnp.float32)
    for n in range(4):
        rim, left, right = (frame(n, part) for part in range(3))
        views = shifted(
            rim, [left[ROWS : ROWS + 1]], [right[ROWS : ROWS + 1]], coef_first, coef_last
        )
        rims.append(views)
        for side, column in enumerate((left[:ROWS], right[:ROWS])):
            above = jnp.concatenate([none, column[: ROWS - 1]], axis=0) * row_coefs[0]
            below = jnp.concatenate([column[1:], none], axis=0) * row_coefs[1]
            columns[side].append((above, column, below))

    def weight(row, a):
        return taps[pl.ds(pl.multiple_of(row * C, 16), C), (2 - a) * C : (3 - a) * C]

    def pair(parts, a, tap):
        return jnp.concatenate([parts[a][tap], parts[a + 1][tap]], axis=0).astype(jnp.bfloat16)

    for side in range(2):
        total = jnp.zeros((2 * ROWS, C), jnp.float32)
        for a in range(3):
            for b in range(3):
                total = total + dot(pair(columns[side], a, b), weight(3 * b + 2 * side, a))
        sides[side] = total
    near = jnp.zeros((2 * COLS, C), jnp.float32)
    first = jnp.where(top, 0, 6)
    for a in range(3):
        for e in range(3):
            near = near + dot(pair(rims, a, e), weight(first + e, a))

    place = lax.broadcasted_iota(jnp.int32, (8, C), 0)
    for f in range(2):
        for k in range(ROWS // 2):
            block = sums[f, k * PAIR : (k + 1) * PAIR]
            parts = []
            for n in range(2):
                row = 2 * k + n
                values = block[n * COLS : (n + 1) * COLS]
                if row == 0:
                    values = values + jnp.where(top, near[f * COLS : (f + 1) * COLS], 0.0)
                if row == ROWS - 1:
                    values = values + jnp.where(top, 0.0, near[f * COLS : (f + 1) * COLS])
                at = slice(f * ROWS + row, f * ROWS + row + 1)
                parts += [
                    values[:8] + jnp.where(place == 0, sides[0, at], 0.0),
                    values[8:16],
                    values[16:] + jnp.where(place == 7, sides[1, at], 0.0),
                ]
            rows = slice(f * CELLS + k * PAIR, f * CELLS + (k + 1) * PAIR)
            out[rows] = jnp.concatenate(parts, axis=0).astype(jnp.bfloat16)


SMEM, VMEM, HBM = (pl.BlockSpec(memory_space=m) for m in (pltpu.SMEM, pltpu.VMEM, pl.ANY))
COEFS = pltpu.VMEM((2, ROWS, C), jnp.float32)
SPARE = pltpu.VMEM((2, 3, COLS, C), jnp.float32)
STACKED = pltpu.VMEM((2, CELLS, DEPTH), jnp.bfloat16)
PARTIAL = jax.ShapeDtypeStruct((2, CELLS, C), jnp.float32)


def call(kernel, inputs, specs, outputs, scratch, flops, mib):
    many = isinstance(outputs, list)
    return pl.pallas_call(
        kernel,
        in_specs=specs,
        out_specs=[VMEM] * len(outputs) if many else VMEM,
        out_shape=outputs,
        scratch_shapes=scratch,
        compiler_params=pltpu.CompilerParams(vmem_limit_bytes=mib * 2**20),
        cost_estimate=pl.CostEstimate(
            flops=flops, bytes_accessed=8 * 2**20, transcendentals=2 * CELLS * C
        ),
    )(*inputs)


def prepare_kernel(group_slot, tile_row, core, index, rim, sems):
    row = jnp.where(tile_row[0] == 1, 0, ROWS - 1)
    copies = [
        pltpu.make_async_copy(core.at[0, f, row], rim.at[f], sems.at[f]) for f in range(2)
    ]
    for copy in copies:
        copy.start()
    away = [(group_slot[d] - group_slot[0] + 4) % 4 for d in (1, 2, 3)]
    index[0] = (away[0] - 1) * 2 + jnp.where(away[1] > away[2], 1, 0)
    for copy in copies:
        copy.wait()


def prepare(group_slot, tile_row, features):
    return pl.pallas_call(
        prepare_kernel,
        in_specs=[SMEM, SMEM, HBM],
        out_specs=[SMEM, VMEM],
        out_shape=[
            jax.ShapeDtypeStruct((1,), jnp.int32),
            jax.ShapeDtypeStruct((2, COLS, C), jnp.bfloat16),
        ],
        scratch_shapes=[pltpu.SemaphoreType.DMA((2,))],
    )(group_slot, tile_row, features)


def cyclic_order(index):
    place = index // 2 + 1
    others = [p for p in (1, 2, 3) if p != place]
    if index % 2:
        others = others[::-1]
    places = [0, place] + others
    return sorted(range(4), key=lambda d: places[d])


def local(features, group_slot, margins, norm_gain, kernel, conv_bias):
    tiles = lax.axis_size("tile")
    across = tiles // GRID_R
    tile_row = (lax.axis_index("tile") // across).astype(jnp.int32).reshape(1)
    group = lax.axis_index("group").astype(jnp.int32).reshape(1)
    weights = kernel.reshape(3, DEPTH, C)
    index, edge = prepare(group_slot, tile_row, features)
    conv_flops = 2 * 3 * CELLS * DEPTH * C

    def routed(order):
        route = [(order[n], order[(n + 1) % 4]) for n in range(4)]

        def branch(features, edge, margins, tile_row, group_slot, group, gain, weights, bias):
            previous = lax.ppermute(features, "group", route)
            rim = lax.ppermute(edge, "tile", [(t, (t + across) % tiles) for t in range(tiles)])
            stacked, columns, taps = call(
                expand_kernel,
                (margins, features.reshape(2 * CELLS, C), gain, weights),
                [SMEM, VMEM, VMEM, HBM],
                [
                    jax.ShapeDtypeStruct((2, CELLS, DEPTH), jnp.bfloat16),
                    jax.ShapeDtypeStruct((2, 2, ROWS, C), jnp.bfloat16),
                    jax.ShapeDtypeStruct((DEPTH, 3 * C), jnp.bfloat16),
                ],
                [
                    COEFS,
                    SPARE,
                    pltpu.VMEM((2, 2, ROWS, C), jnp.float32),
                    pltpu.SemaphoreType.DMA((3,)),
                ],
                2 * CELLS * DEPTH,
                16,
            )
            own = call(own_kernel, (stacked, taps), [VMEM] * 2, PARTIAL, [], conv_flops, 16)
            spare = jnp.zeros((2, COLS - ROWS - 1, C), jnp.bfloat16)
            first, last = (
                jnp.concatenate([columns[side], rim[:, at : at + 1], spare], axis=1)
                for side, at in ((0, 0), (1, COLS - 1))
            )
            inner = [t for t in range(tiles) if t % across != across - 1]
            left = lax.ppermute(last, "tile", [(t, t + 1) for t in inner])
            right = lax.ppermute(first, "tile", [(t + 1, t) for t in inner])
            halo = jnp.stack([rim, left, right])
            halo_previous = lax.ppermute(halo, "group", route)
            sums = call(
                previous_kernel,
                (margins, group_slot, group, previous.reshape(2 * CELLS, C), gain, taps, own, bias),
                [SMEM, SMEM, SMEM, VMEM, VMEM, VMEM, VMEM, VMEM],
                PARTIAL,
                [COEFS, SPARE, STACKED],
                conv_flops,
                16,
            )
            return call(
                join_kernel,
                (margins, tile_row, group_slot, group, halo, halo_previous, gain, taps, sums),
                [SMEM] * 4 + [VMEM] * 5,
                jax.ShapeDtypeStruct((2 * CELLS, C), jnp.bfloat16),
                [COEFS, pltpu.VMEM((2, 2 * ROWS, C), jnp.float32)],
                2 * 3 * 9 * 40 * C * C,
                16,
            )

        return branch

    decoded = lax.switch(
        index[0],
        [routed(cyclic_order(n)) for n in range(6)],
        features,
        edge,
        margins,
        tile_row,
        group_slot,
        group,
        norm_gain,
        weights,
        conv_bias,
    )
    return decoded.reshape(1, 2, ROWS, COLS, C)


def solution(mesh):
    return jax.shard_map(
        local,
        mesh=mesh,
        in_specs=(
            P(("video", "tile"), "group", None, None, None),
            P(),
            P("tile", None),
            P(),
            P(),
            P(),
        ),
        out_specs=P(("video", "tile"), "group", None, None, None),
        check_vma=False,
    )
```

```python
import jax
import jax.numpy as jnp
from jax import lax
from jax.experimental import pallas as pl
from jax.experimental.pallas import tpu as pltpu
from jax.sharding import PartitionSpec as P

GRID_R = 2
ROWS, COLS, C = 16, 24, 384
CELLS = ROWS * COLS
PAIR = 2 * COLS
DEPTH = 9 * C


def activated(values, half_gain):
    inv_norm = lax.rsqrt(jnp.mean(values * values, axis=-1, keepdims=True) + 1e-06)
    half = values * inv_norm * half_gain
    silu = half + half * jnp.tanh(half)
    return silu.astype(jnp.bfloat16).astype(jnp.float32)


def blend_coef(position, tap, core, near, far):
    source = position + (tap - 1)
    near_f, far_f = near.astype(jnp.float32), far.astype(jnp.float32)
    weight_near = jnp.maximum(near - position, 0).astype(jnp.float32) / (near_f + 1.0)
    weight_far = jnp.maximum(far + 1 - core + position, 0).astype(jnp.float32) / (far_f + 1.0)
    kept = jnp.where(source < near, weight_near, 0.0)
    kept = kept + jnp.where(source >= core - far, weight_far, 0.0)
    kept = kept + jnp.where((source >= -near) & (source < core + far), 1.0, 0.0)
    return kept / (weight_near + 1.0 + weight_far)


def shifted(block, left, right, coef_first, coef_last):
    size = block.shape[0]
    place = lax.broadcasted_iota(jnp.int32, (8, C), 0)
    before = pltpu.roll(block, 1, 0)
    after = pltpu.roll(block, size - 1, 0)
    before_parts, after_parts = [], []
    for n in range(size // COLS):
        first, middle, last = (slice(n * COLS + at, n * COLS + at + 8) for at in (0, 8, 16))
        before_parts += [
            jnp.where(place == 0, left[n], before[first]),
            before[middle],
            before[last] * coef_first,
        ]
        after_parts += [
            after[first] * coef_last,
            after[middle],
            jnp.where(place == 7, right[n], after[last]),
        ]
    return jnp.concatenate(before_parts, axis=0), block, jnp.concatenate(after_parts, axis=0)


def expand(margins, core, gain, row_coefs, spare, stacked, columns):
    fill_row_coefs(margins, row_coefs)
    coef_first, coef_last = column_coefs(margins)
    half_gain = 0.5 * gain
    zeros = [jnp.zeros((1, C), jnp.float32)] * 4
    spare[...] = jnp.zeros_like(spare)

    def lanes(b, e):
        return slice((3 * b + e) * C, (3 * b + e + 1) * C)

    def put(f, k, b, e, values, scale):
        if scale:
            values = [
                p * row_coefs[b // 2, pl.ds(2 * k + n, 1), :] for n, p in enumerate(values)
            ]
        values = jnp.concatenate(values, axis=0).astype(jnp.bfloat16)
        stacked[f, pl.ds(pl.multiple_of(k * PAIR, 16), PAIR), lanes(b, e)] = values

    def two_rows(k, _):
        blocks = [
            core[pl.ds(pl.multiple_of(f * CELLS + k * PAIR, 16), PAIR), :].astype(jnp.float32)
            for f in range(2)
        ]
        if columns is not None:
            for f in range(2):
                for n in range(2):
                    first, last = n * COLS, n * COLS + COLS - 1
                    columns[0, f, pl.ds(2 * k + n, 1), :] = blocks[f][first : first + 1]
                    columns[1, f, pl.ds(2 * k + n, 1), :] = blocks[f][last : last + 1]
        block = activated(jnp.concatenate(blocks, axis=0), half_gain)
        views = shifted(block, zeros, zeros, coef_first, coef_last)
        for f in range(2):
            for e in range(3):
                rows = [views[e][(2 * f + n) * COLS : (2 * f + n + 1) * COLS] for n in range(2)]
                put(f, k, 1, e, rows, False)
                odd = [spare[f, e], rows[0]]
                spare[f, e] = rows[1]
                put(f, k, 0, e, odd, True)
                put(f, jnp.maximum(k - 1, 0), 2, e, odd, True)
        return 0

    lax.fori_loop(0, ROWS // 2, two_rows, 0)
    for f in range(2):
        for e in range(3):
            put(f, ROWS // 2 - 1, 2, e, [spare[f, e], jnp.zeros((COLS, C), jnp.float32)], False)


def fill_row_coefs(margins, row_coefs):
    row = lax.broadcasted_iota(jnp.int32, (ROWS, C), 0)
    for n, b in enumerate((0, 2)):
        row_coefs[n] = blend_coef(row, b, ROWS, margins[0, 2], margins[0, 3])


def column_coefs(margins):
    place = lax.broadcasted_iota(jnp.int32, (8, C), 0)
    coef_first = blend_coef(place + (COLS - 8), 0, COLS, margins[0, 0], margins[0, 1])
    coef_last = blend_coef(place, 2, COLS, margins[0, 0], margins[0, 1])
    return coef_first, coef_last


def dot(a, b):
    return jnp.dot(a, b, preferred_element_type=jnp.float32)


def weights_of(weights, times):
    return jnp.concatenate([weights[a] for a in times], axis=1)


def expand_kernel(
    margins, core, gain, weights, stacked, columns, taps, row_coefs, spare, cells, sems
):
    copies = [
        pltpu.make_async_copy(weights.at[2 - n], taps.at[:, pl.ds(n * C, C)], sems.at[n])
        for n in range(3)
    ]
    for copy in copies:
        copy.start()
    expand(margins, core, gain[...].reshape(1, C), row_coefs, spare, stacked, cells)
    columns[...] = cells[...].astype(jnp.bfloat16)
    for copy in copies:
        copy.wait()


def own_kernel(stacked, taps, own):
    third = DEPTH // 3
    own[...] = jnp.zeros_like(own)

    def part(n, _):
        rows = pl.ds(pl.multiple_of((n // 3) * 192, 16), 192)
        depth = pl.ds(pl.multiple_of((n % 3) * third, 128), third)
        both = dot(stacked[0, rows, depth], taps[depth, : 2 * C])
        own[0, rows, :] += both[:, :C]
        own[1, rows, :] += both[:, C:] + dot(stacked[1, rows, depth], taps[depth, :C])
        return 0

    lax.fori_loop(0, 3 * (CELLS // 192), part, 0)


def previous_kernel(
    margins, group_slot, group, core, gain, taps, own, bias, sums, row_coefs, spare, stacked
):
    bias = bias[...].reshape(1, C)
    gain = jnp.where(group_slot[group[0]] > 0, gain[...].reshape(1, C), 0.0)
    expand(margins, core, gain, row_coefs, spare, stacked, None)

    def part(n, _):
        rows = pl.ds(pl.multiple_of(n * 128, 16), 128)
        both = dot(stacked[1, rows, :], taps[:, C:])
        last = dot(stacked[0, rows, :], taps[:, 2 * C :])
        sums[0, rows, :] = own[0, rows, :] + bias + both[:, :C] + last
        sums[1, rows, :] = own[1, rows, :] + bias + both[:, C:]
        return 0

    lax.fori_loop(0, CELLS // 128, part, 0)


def join_kernel(
    margins,
    tile_row,
    group_slot,
    group,
    halo,
    halo_previous,
    gain,
    taps,
    sums,
    out,
    row_coefs,
    sides,
    near,
    columns,
    rims,
):
    fill_row_coefs(margins, row_coefs)
    coef_first, coef_last = column_coefs(margins)
    half_gain = 0.5 * gain[...].reshape(1, C)
    half_previous = jnp.where(group_slot[group[0]] > 0, half_gain, 0.0)
    top = tile_row[0] == 1
    none = jnp.zeros((1, C), jnp.float32)

    def frames(f, _):
        for n, (source, scale) in enumerate(((halo_previous, half_previous), (halo, half_gain))):
            rim, left, right = (
                activated(source[part, f].astype(jnp.float32), scale) for part in range(3)
            )
            views = shifted(
                rim, [left[ROWS : ROWS + 1]], [right[ROWS : ROWS + 1]], coef_first, coef_last
            )
            at = 2 * n + f
            for e in range(3):
                values = jnp.concatenate([views[e], jnp.zeros((8, C), jnp.float32)], axis=0)
                rims[e, pl.ds(pl.multiple_of(at * 32, 32), 32), :] = values.astype(jnp.bfloat16)
            for side, column in enumerate((left[:ROWS], right[:ROWS])):
                above = jnp.concatenate([none, column[: ROWS - 1]], axis=0) * row_coefs[0]
                below = jnp.concatenate([column[1:], none], axis=0) * row_coefs[1]
                for b, values in enumerate((above, column, below)):
                    rows = pl.ds(pl.multiple_of(at * ROWS, 16), ROWS)
                    columns[3 * side + b, rows, :] = values.astype(jnp.bfloat16)
        return 0

    lax.fori_loop(0, 2, frames, 0)
    sides[...] = jnp.zeros_like(sides)
    near[...] = jnp.zeros_like(near)
    first = jnp.where(top, 0, 6)

    def times(a, _):
        lanes = pl.ds(pl.multiple_of((2 - a) * C, 128), C)

        def weight(row):
            return taps[pl.ds(pl.multiple_of(row * C, 16), C), lanes]

        rows = pl.ds(pl.multiple_of(a * ROWS, 16), 2 * ROWS)
        for side in range(2):
            sides[side] += sum(
                dot(columns[3 * side + b, rows, :], weight(3 * b + 2 * side)) for b in range(3)
            )
        rows = pl.ds(pl.multiple_of(a * 32, 32), 64)
        near[...] += sum(dot(rims[e, rows, :], weight(first + e)) for e in range(3))
        return 0

    lax.fori_loop(0, 3, times, 0)
    place = lax.broadcasted_iota(jnp.int32, (8, C), 0)

    def two_rows(k, _):
        for f in range(2):
            block = sums[f, pl.ds(pl.multiple_of(k * PAIR, 16), PAIR), :]
            beside = near[32 * f : 32 * f + COLS]
            parts = []
            for n, here in enumerate((top & (k == 0), ~top & (k == ROWS // 2 - 1))):
                values = block[n * COLS : (n + 1) * COLS] + jnp.where(here, beside, 0.0)
                at = pl.ds(f * ROWS + 2 * k + n, 1)
                parts += [
                    values[:8] + jnp.where(place == 0, sides[0, at, :], 0.0),
                    values[8:16],
                    values[16:] + jnp.where(place == 7, sides[1, at, :], 0.0),
                ]
            rows = pl.ds(pl.multiple_of(f * CELLS + k * PAIR, 16), PAIR)
            out[rows, :] = jnp.concatenate(parts, axis=0).astype(jnp.bfloat16)
        return 0

    lax.fori_loop(0, ROWS // 2, two_rows, 0)


SMEM, VMEM, HBM = (pl.BlockSpec(memory_space=m) for m in (pltpu.SMEM, pltpu.VMEM, pl.ANY))
COEFS = pltpu.VMEM((2, ROWS, C), jnp.float32)
SPARE = pltpu.VMEM((2, 3, COLS, C), jnp.float32)
STACKED = pltpu.VMEM((2, CELLS, DEPTH), jnp.bfloat16)
PARTIAL = jax.ShapeDtypeStruct((2, CELLS, C), jnp.float32)


def call(kernel, inputs, specs, outputs, scratch, flops, mib):
    many = isinstance(outputs, list)
    return pl.pallas_call(
        kernel,
        in_specs=specs,
        out_specs=[VMEM] * len(outputs) if many else VMEM,
        out_shape=outputs,
        scratch_shapes=scratch,
        compiler_params=pltpu.CompilerParams(vmem_limit_bytes=mib * 2**20),
        cost_estimate=pl.CostEstimate(
            flops=flops, bytes_accessed=8 * 2**20, transcendentals=2 * CELLS * C
        ),
    )(*inputs)


def prepare_kernel(group_slot, tile_row, core, index, rim, sems):
    row = jnp.where(tile_row[0] == 1, 0, ROWS - 1)
    copies = [
        pltpu.make_async_copy(core.at[0, f, row], rim.at[f], sems.at[f]) for f in range(2)
    ]
    for copy in copies:
        copy.start()
    away = [(group_slot[d] - group_slot[0] + 4) % 4 for d in (1, 2, 3)]
    index[0] = (away[0] - 1) * 2 + jnp.where(away[1] > away[2], 1, 0)
    for copy in copies:
        copy.wait()


def prepare(group_slot, tile_row, features):
    return pl.pallas_call(
        prepare_kernel,
        in_specs=[SMEM, SMEM, HBM],
        out_specs=[SMEM, VMEM],
        out_shape=[
            jax.ShapeDtypeStruct((1,), jnp.int32),
            jax.ShapeDtypeStruct((2, COLS, C), jnp.bfloat16),
        ],
        scratch_shapes=[pltpu.SemaphoreType.DMA((2,))],
    )(group_slot, tile_row, features)


def cyclic_order(index):
    place = index // 2 + 1
    others = [p for p in (1, 2, 3) if p != place]
    if index % 2:
        others = others[::-1]
    places = [0, place] + others
    return sorted(range(4), key=lambda d: places[d])


def local(features, group_slot, margins, norm_gain, kernel, conv_bias):
    tiles = lax.axis_size("tile")
    across = tiles // GRID_R
    tile_row = (lax.axis_index("tile") // across).astype(jnp.int32).reshape(1)
    group = lax.axis_index("group").astype(jnp.int32).reshape(1)
    weights = kernel.reshape(3, DEPTH, C)
    index, edge = prepare(group_slot, tile_row, features)
    conv_flops = 2 * 3 * CELLS * DEPTH * C

    def routed(order):
        route = [(order[n], order[(n + 1) % 4]) for n in range(4)]

        def branch(features, edge, margins, tile_row, group_slot, group, gain, weights, bias):
            previous = lax.ppermute(features, "group", route)
            rim = lax.ppermute(edge, "tile", [(t, (t + across) % tiles) for t in range(tiles)])
            stacked, columns, taps = call(
                expand_kernel,
                (margins, features.reshape(2 * CELLS, C), gain, weights),
                [SMEM, VMEM, VMEM, HBM],
                [
                    jax.ShapeDtypeStruct((2, CELLS, DEPTH), jnp.bfloat16),
                    jax.ShapeDtypeStruct((2, 2, ROWS, C), jnp.bfloat16),
                    jax.ShapeDtypeStruct((DEPTH, 3 * C), jnp.bfloat16),
                ],
                [
                    COEFS,
                    SPARE,
                    pltpu.VMEM((2, 2, ROWS, C), jnp.float32),
                    pltpu.SemaphoreType.DMA((3,)),
                ],
                2 * CELLS * DEPTH,
                16,
            )
            own = call(own_kernel, (stacked, taps), [VMEM] * 2, PARTIAL, [], conv_flops, 16)
            spare = jnp.zeros((2, COLS - ROWS - 1, C), jnp.bfloat16)
            first, last = (
                jnp.concatenate([columns[side], rim[:, at : at + 1], spare], axis=1)
                for side, at in ((0, 0), (1, COLS - 1))
            )
            inner = [t for t in range(tiles) if t % across != across - 1]
            left = lax.ppermute(last, "tile", [(t, t + 1) for t in inner])
            right = lax.ppermute(first, "tile", [(t + 1, t) for t in inner])
            halo = jnp.stack([rim, left, right])
            halo_previous = lax.ppermute(halo, "group", route)
            sums = call(
                previous_kernel,
                (margins, group_slot, group, previous.reshape(2 * CELLS, C), gain, taps, own, bias),
                [SMEM, SMEM, SMEM, VMEM, VMEM, VMEM, VMEM, VMEM],
                PARTIAL,
                [COEFS, SPARE, STACKED],
                conv_flops,
                16,
            )
            return call(
                join_kernel,
                (margins, tile_row, group_slot, group, halo, halo_previous, gain, taps, sums),
                [SMEM] * 4 + [VMEM] * 5,
                jax.ShapeDtypeStruct((2 * CELLS, C), jnp.bfloat16),
                [
                    COEFS,
                    pltpu.VMEM((2, 2 * ROWS, C), jnp.float32),
                    pltpu.VMEM((64, C), jnp.float32),
                    pltpu.VMEM((6, 4 * ROWS, C), jnp.bfloat16),
                    pltpu.VMEM((3, 4 * 32, C), jnp.bfloat16),
                ],
                2 * 3 * 9 * 40 * C * C,
                16,
            )

        return branch

    decoded = lax.switch(
        index[0],
        [routed(cyclic_order(n)) for n in range(6)],
        features,
        edge,
        margins,
        tile_row,
        group_slot,
        group,
        norm_gain,
        weights,
        conv_bias,
    )
    return decoded.reshape(1, 2, ROWS, COLS, C)


def solution(mesh):
    return jax.shard_map(
        local,
        mesh=mesh,
        in_specs=(
            P(("video", "tile"), "group", None, None, None),
            P(),
            P("tile", None),
            P(),
            P(),
            P(),
        ),
        out_specs=P(("video", "tile"), "group", None, None, None),
        check_vma=False,
    )
```

```python
import jax
import jax.numpy as jnp
from jax import lax
from jax.experimental import pallas as pl
from jax.experimental.pallas import tpu as pltpu
from jax.sharding import PartitionSpec as P

GRID_R = 2
ROWS, COLS, C = 16, 24, 384
CELLS = ROWS * COLS
PAIR = 2 * COLS
DEPTH = 9 * C


def activated(values, half_gain):
    inv_norm = lax.rsqrt(jnp.mean(values * values, axis=-1, keepdims=True) + 1e-06)
    half = values * inv_norm * half_gain
    silu = half + half * jnp.tanh(half)
    return silu.astype(jnp.bfloat16).astype(jnp.float32)


def blend_coef(position, tap, core, near, far):
    source = position + (tap - 1)
    near_f, far_f = near.astype(jnp.float32), far.astype(jnp.float32)
    weight_near = jnp.maximum(near - position, 0).astype(jnp.float32) / (near_f + 1.0)
    weight_far = jnp.maximum(far + 1 - core + position, 0).astype(jnp.float32) / (far_f + 1.0)
    kept = jnp.where(source < near, weight_near, 0.0)
    kept = kept + jnp.where(source >= core - far, weight_far, 0.0)
    kept = kept + jnp.where((source >= -near) & (source < core + far), 1.0, 0.0)
    return kept / (weight_near + 1.0 + weight_far)


def shifted(block, left, right, coef_first, coef_last):
    size = block.shape[0]
    place = lax.broadcasted_iota(jnp.int32, (8, C), 0)
    before = pltpu.roll(block, 1, 0)
    after = pltpu.roll(block, size - 1, 0)
    before_parts, after_parts = [], []
    for n in range(size // COLS):
        first, middle, last = (slice(n * COLS + at, n * COLS + at + 8) for at in (0, 8, 16))
        before_parts += [
            jnp.where(place == 0, left[n], before[first]),
            before[middle],
            before[last] * coef_first,
        ]
        after_parts += [
            after[first] * coef_last,
            after[middle],
            jnp.where(place == 7, right[n], after[last]),
        ]
    return jnp.concatenate(before_parts, axis=0), block, jnp.concatenate(after_parts, axis=0)


def expand(margins, core, gain, row_coefs, spare, ahead, stacked, columns):
    fill_row_coefs(margins, row_coefs)
    coef_first, coef_last = column_coefs(margins)
    half_gain = 0.5 * gain
    zeros = [jnp.zeros((1, C), jnp.float32)] * 4
    spare[...] = jnp.zeros_like(spare)

    def lanes(b, e):
        return slice((3 * b + e) * C, (3 * b + e + 1) * C)

    def put(f, k, b, e, values, scale):
        if scale:
            values = [
                p * row_coefs[b // 2, pl.ds(2 * k + n, 1), :] for n, p in enumerate(values)
            ]
        values = jnp.concatenate(values, axis=0).astype(jnp.bfloat16)
        stacked[f][pl.ds(pl.multiple_of(k * PAIR, 16), PAIR), lanes(b, e)] = values

    ahead[...] = jnp.zeros_like(ahead)

    def two_rows(step, _):
        block = ahead[...]
        after = jnp.minimum(step, ROWS // 2 - 1)
        blocks = [
            core[pl.ds(pl.multiple_of(f * CELLS + after * PAIR, 16), PAIR), :].astype(jnp.float32)
            for f in range(2)
        ]
        if columns is not None:
            for f in range(2):
                for n in range(2):
                    first, last = n * COLS, n * COLS + COLS - 1
                    columns[0, f, pl.ds(2 * after + n, 1), :] = blocks[f][first : first + 1]
                    columns[1, f, pl.ds(2 * after + n, 1), :] = blocks[f][last : last + 1]
        ahead[...] = activated(jnp.concatenate(blocks, axis=0), half_gain)
        k = jnp.maximum(step - 1, 0)
        views = shifted(block, zeros, zeros, coef_first, coef_last)
        for f in range(2):
            for e in range(3):
                rows = [views[e][(2 * f + n) * COLS : (2 * f + n + 1) * COLS] for n in range(2)]
                put(f, k, 1, e, rows, False)
                odd = [spare[f, e], rows[0]]
                spare[f, e] = rows[1]
                put(f, k, 0, e, odd, True)
                put(f, jnp.maximum(k - 1, 0), 2, e, odd, True)
        return 0

    lax.fori_loop(0, ROWS // 2 + 1, two_rows, 0)
    for f in range(2):
        for e in range(3):
            put(f, ROWS // 2 - 1, 2, e, [spare[f, e], jnp.zeros((COLS, C), jnp.float32)], False)


def fill_row_coefs(margins, row_coefs):
    row = lax.broadcasted_iota(jnp.int32, (ROWS, C), 0)
    for n, b in enumerate((0, 2)):
        row_coefs[n] = blend_coef(row, b, ROWS, margins[0, 2], margins[0, 3])


def column_coefs(margins):
    place = lax.broadcasted_iota(jnp.int32, (8, C), 0)
    coef_first = blend_coef(place + (COLS - 8), 0, COLS, margins[0, 0], margins[0, 1])
    coef_last = blend_coef(place, 2, COLS, margins[0, 0], margins[0, 1])
    return coef_first, coef_last


def dot(a, b):
    return jnp.dot(a, b, preferred_element_type=jnp.float32)


def weights_of(weights, times):
    return jnp.concatenate([weights[a] for a in times], axis=1)


def add_products(to, rows_of, weights_of):
    third = DEPTH // 3

    def part(n, _):
        rows = pl.ds(pl.multiple_of((n // 3) * 192, 16), 192)
        depth = pl.ds(pl.multiple_of((n % 3) * third, 128), third)
        to(rows, dot(rows_of(rows, depth), weights_of(depth)))
        return 0

    lax.fori_loop(0, 3 * (CELLS // 192), part, 0)


def expand_own_kernel(
    margins,
    core,
    gain,
    weights,
    early,
    own,
    columns,
    taps,
    row_coefs,
    spare,
    ahead,
    cells,
    late,
    sems,
):
    copies = [
        pltpu.make_async_copy(weights.at[2 - n], taps.at[:, pl.ds(n * C, C)], sems.at[n])
        for n in range(3)
    ]
    for copy in copies:
        copy.start()
    own[...] = jnp.zeros_like(own)
    expand(margins, core, gain[...].reshape(1, C), row_coefs, spare, ahead, (early, late), cells)
    columns[...] = cells[...].astype(jnp.bfloat16)
    copies[0].wait()

    def add(rows, product):
        own[rows, :] += product

    add_products(add, lambda rows, depth: late[rows, depth], lambda depth: taps[depth, :C])
    for copy in copies[1:]:
        copy.wait()


def own_kernel(early, taps, late, own):
    own[0] = jnp.zeros_like(late)
    own[1] = late[...]

    def add(rows, product):
        own[0, rows, :] += product[:, :C]
        own[1, rows, :] += product[:, C:]

    add_products(add, lambda rows, depth: early[rows, depth], lambda depth: taps[depth, : 2 * C])


def expand_previous_kernel(
    margins, group_slot, group, core, gain, stacked, row_coefs, spare, ahead
):
    gain = jnp.where(group_slot[group[0]] > 0, gain[...].reshape(1, C), 0.0)
    expand(margins, core, gain, row_coefs, spare, ahead, (stacked.at[0], stacked.at[1]), None)


def previous_kernel(stacked, taps, own, bias, sums):
    bias = bias[...].reshape(1, C)

    def part(n, _):
        rows = pl.ds(pl.multiple_of(n * 128, 16), 128)
        both = dot(stacked[1, rows, :], taps[:, C:])
        last = dot(stacked[0, rows, :], taps[:, 2 * C :])
        sums[0, rows, :] = own[0, rows, :] + bias + both[:, :C] + last
        sums[1, rows, :] = own[1, rows, :] + bias + both[:, C:]
        return 0

    lax.fori_loop(0, CELLS // 128, part, 0)


def join_kernel(
    margins,
    tile_row,
    group_slot,
    group,
    halo,
    halo_previous,
    gain,
    taps,
    sums,
    out,
    row_coefs,
    sides,
    near,
    columns,
    rims,
):
    fill_row_coefs(margins, row_coefs)
    coef_first, coef_last = column_coefs(margins)
    half_gain = 0.5 * gain[...].reshape(1, C)
    half_previous = jnp.where(group_slot[group[0]] > 0, half_gain, 0.0)
    top = tile_row[0] == 1
    none = jnp.zeros((1, C), jnp.float32)

    def frames(f, _):
        for n, (source, scale) in enumerate(((halo_previous, half_previous), (halo, half_gain))):
            rim, left, right = (
                activated(source[part, f].astype(jnp.float32), scale) for part in range(3)
            )
            views = shifted(
                rim, [left[ROWS : ROWS + 1]], [right[ROWS : ROWS + 1]], coef_first, coef_last
            )
            at = 2 * n + f
            for e in range(3):
                values = jnp.concatenate([views[e], jnp.zeros((8, C), jnp.float32)], axis=0)
                rims[e, pl.ds(pl.multiple_of(at * 32, 32), 32), :] = values.astype(jnp.bfloat16)
            for side, column in enumerate((left[:ROWS], right[:ROWS])):
                above = jnp.concatenate([none, column[: ROWS - 1]], axis=0) * row_coefs[0]
                below = jnp.concatenate([column[1:], none], axis=0) * row_coefs[1]
                for b, values in enumerate((above, column, below)):
                    rows = pl.ds(pl.multiple_of(at * ROWS, 16), ROWS)
                    columns[3 * side + b, rows, :] = values.astype(jnp.bfloat16)
        return 0

    lax.fori_loop(0, 2, frames, 0)
    sides[...] = jnp.zeros_like(sides)
    near[...] = jnp.zeros_like(near)
    first = jnp.where(top, 0, 6)

    def times(a, _):
        lanes = pl.ds(pl.multiple_of((2 - a) * C, 128), C)

        def weight(row):
            return taps[pl.ds(pl.multiple_of(row * C, 16), C), lanes]

        rows = pl.ds(pl.multiple_of(a * ROWS, 16), 2 * ROWS)
        for side in range(2):
            sides[side] += sum(
                dot(columns[3 * side + b, rows, :], weight(3 * b + 2 * side)) for b in range(3)
            )
        rows = pl.ds(pl.multiple_of(a * 32, 32), 64)
        near[...] += sum(dot(rims[e, rows, :], weight(first + e)) for e in range(3))
        return 0

    lax.fori_loop(0, 3, times, 0)
    place = lax.broadcasted_iota(jnp.int32, (8, C), 0)

    def two_rows(k, _):
        for f in range(2):
            block = sums[f, pl.ds(pl.multiple_of(k * PAIR, 16), PAIR), :]
            beside = near[32 * f : 32 * f + COLS]
            parts = []
            for n, here in enumerate((top & (k == 0), ~top & (k == ROWS // 2 - 1))):
                values = block[n * COLS : (n + 1) * COLS] + jnp.where(here, beside, 0.0)
                at = pl.ds(f * ROWS + 2 * k + n, 1)
                parts += [
                    values[:8] + jnp.where(place == 0, sides[0, at, :], 0.0),
                    values[8:16],
                    values[16:] + jnp.where(place == 7, sides[1, at, :], 0.0),
                ]
            rows = pl.ds(pl.multiple_of(f * CELLS + k * PAIR, 16), PAIR)
            out[rows, :] = jnp.concatenate(parts, axis=0).astype(jnp.bfloat16)
        return 0

    lax.fori_loop(0, ROWS // 2, two_rows, 0)


SMEM, VMEM, HBM = (pl.BlockSpec(memory_space=m) for m in (pltpu.SMEM, pltpu.VMEM, pl.ANY))
COEFS = pltpu.VMEM((2, ROWS, C), jnp.float32)
SPARE = pltpu.VMEM((2, 3, COLS, C), jnp.float32)
AHEAD = pltpu.VMEM((2 * PAIR, C), jnp.float32)
PARTIAL = jax.ShapeDtypeStruct((2, CELLS, C), jnp.float32)


def call(kernel, inputs, specs, outputs, scratch, flops, mib):
    many = isinstance(outputs, list)
    return pl.pallas_call(
        kernel,
        in_specs=specs,
        out_specs=[VMEM] * len(outputs) if many else VMEM,
        out_shape=outputs,
        scratch_shapes=scratch,
        compiler_params=pltpu.CompilerParams(vmem_limit_bytes=mib * 2**20),
        cost_estimate=pl.CostEstimate(
            flops=flops, bytes_accessed=flops // 2**10, transcendentals=0
        ),
    )(*inputs)


def prepare_kernel(core, group_slot, tile_row, index, rim, slots, sems):
    row = jnp.where(tile_row[0] == 1, 0, ROWS - 1)
    copies = [pltpu.make_async_copy(group_slot, slots, sems.at[2])] + [
        pltpu.make_async_copy(core.at[0, f, row], rim.at[f], sems.at[f]) for f in range(2)
    ]
    for copy in copies:
        copy.start()
    copies[0].wait()
    away = [(slots[d] - slots[0] + 4) % 4 for d in (1, 2, 3)]
    index[0] = (away[0] - 1) * 2 + jnp.where(away[1] > away[2], 1, 0)
    for copy in copies[1:]:
        copy.wait()


def prepare(features, group_slot, tile_row):
    return pl.pallas_call(
        prepare_kernel,
        in_specs=[HBM, HBM, SMEM],
        out_specs=[SMEM, VMEM],
        out_shape=[
            jax.ShapeDtypeStruct((1,), jnp.int32),
            jax.ShapeDtypeStruct((2, COLS, C), jnp.bfloat16),
        ],
        scratch_shapes=[pltpu.SMEM((4,), jnp.int32), pltpu.SemaphoreType.DMA((3,))],
    )(features, group_slot, tile_row)


def cyclic_order(index):
    place = index // 2 + 1
    others = [p for p in (1, 2, 3) if p != place]
    if index % 2:
        others = others[::-1]
    places = [0, place] + others
    return sorted(range(4), key=lambda d: places[d])


def local(features, group_slot, margins, norm_gain, kernel, conv_bias):
    tiles = lax.axis_size("tile")
    across = tiles // GRID_R
    tile_row = (lax.axis_index("tile") // across).astype(jnp.int32).reshape(1)
    group = lax.axis_index("group").astype(jnp.int32).reshape(1)
    weights = kernel.reshape(3, DEPTH, C)
    index, edge = prepare(features, group_slot, tile_row)
    conv_flops = 2 * 3 * CELLS * DEPTH * C

    def routed(order):
        route = [(order[n], order[(n + 1) % 4]) for n in range(4)]

        def branch(features, edge, margins, tile_row, group_slot, group, gain, weights, bias):
            previous = lax.ppermute(features, "group", route)
            rim = lax.ppermute(edge, "tile", [(t, (t + across) % tiles) for t in range(tiles)])
            early, late, columns, taps = call(
                expand_own_kernel,
                (margins, features.reshape(2 * CELLS, C), gain, weights),
                [SMEM, VMEM, VMEM, HBM],
                [
                    jax.ShapeDtypeStruct((CELLS, DEPTH), jnp.bfloat16),
                    jax.ShapeDtypeStruct((CELLS, C), jnp.float32),
                    jax.ShapeDtypeStruct((2, 2, ROWS, C), jnp.bfloat16),
                    jax.ShapeDtypeStruct((DEPTH, 3 * C), jnp.bfloat16),
                ],
                [
                    COEFS,
                    SPARE,
                    AHEAD,
                    pltpu.VMEM((2, 2, ROWS, C), jnp.float32),
                    pltpu.VMEM((CELLS, DEPTH), jnp.bfloat16),
                    pltpu.SemaphoreType.DMA((3,)),
                ],
                conv_flops // 3,
                8,
            )
            spare = jnp.zeros((2, COLS - ROWS - 1, C), jnp.bfloat16)
            first, last = (
                jnp.concatenate([columns[side], rim[:, at : at + 1], spare], axis=1)
                for side, at in ((0, 0), (1, COLS - 1))
            )
            inner = [t for t in range(tiles) if t % across != across - 1]
            left = lax.ppermute(last, "tile", [(t, t + 1) for t in inner])
            right = lax.ppermute(first, "tile", [(t + 1, t) for t in inner])
            own = call(
                own_kernel, (early, taps, late), [VMEM] * 3, PARTIAL, [], CELLS, 8
            )
            stacked = call(
                expand_previous_kernel,
                (margins, group_slot, group, previous.reshape(2 * CELLS, C), gain),
                [SMEM, SMEM, SMEM, VMEM, VMEM],
                jax.ShapeDtypeStruct((2, CELLS, DEPTH), jnp.bfloat16),
                [COEFS, SPARE, AHEAD],
                conv_flops // 3,
                8,
            )
            halo = jnp.stack([rim, left, right])
            halo_previous = lax.ppermute(halo, "group", route)
            sums = call(
                previous_kernel, (stacked, taps, own, bias), [VMEM] * 4, PARTIAL, [], conv_flops, 8
            )
            return call(
                join_kernel,
                (margins, tile_row, group_slot, group, halo, halo_previous, gain, taps, sums),
                [SMEM] * 4 + [VMEM] * 5,
                jax.ShapeDtypeStruct((2 * CELLS, C), jnp.bfloat16),
                [
                    COEFS,
                    pltpu.VMEM((2, 2 * ROWS, C), jnp.float32),
                    pltpu.VMEM((64, C), jnp.float32),
                    pltpu.VMEM((6, 4 * ROWS, C), jnp.bfloat16),
                    pltpu.VMEM((3, 4 * 32, C), jnp.bfloat16),
                ],
                2 * 3 * 9 * 40 * C * C,
                8,
            )

        return branch

    decoded = lax.switch(
        index[0],
        [routed(cyclic_order(n)) for n in range(6)],
        features,
        edge,
        margins,
        tile_row,
        group_slot,
        group,
        norm_gain,
        weights,
        conv_bias,
    )
    return decoded.reshape(1, 2, ROWS, COLS, C)


def solution(mesh):
    return jax.shard_map(
        local,
        mesh=mesh,
        in_specs=(
            P(("video", "tile"), "group", None, None, None),
            P(),
            P("tile", None),
            P(),
            P(),
            P(),
        ),
        out_specs=P(("video", "tile"), "group", None, None, None),
        check_vma=False,
    )
```

```python
import jax
import jax.numpy as jnp
from jax import lax
from jax.experimental import pallas as pl
from jax.experimental.pallas import tpu as pltpu
from jax.sharding import PartitionSpec as P

GRID_R = 2
ROWS, COLS, C = 16, 24, 384
CELLS = ROWS * COLS
PAIR = 2 * COLS
DEPTH = 9 * C


def activated(values, half_gain):
    inv_norm = lax.rsqrt(jnp.mean(values * values, axis=-1, keepdims=True) + 1e-06)
    half = values * inv_norm * half_gain
    silu = half + half * jnp.tanh(half)
    return silu.astype(jnp.bfloat16).astype(jnp.float32)


def blend_coef(position, tap, core, near, far):
    source = position + (tap - 1)
    near_f, far_f = near.astype(jnp.float32), far.astype(jnp.float32)
    weight_near = jnp.maximum(near - position, 0).astype(jnp.float32) / (near_f + 1.0)
    weight_far = jnp.maximum(far + 1 - core + position, 0).astype(jnp.float32) / (far_f + 1.0)
    kept = jnp.where(source < near, weight_near, 0.0)
    kept = kept + jnp.where(source >= core - far, weight_far, 0.0)
    kept = kept + jnp.where((source >= -near) & (source < core + far), 1.0, 0.0)
    return kept / (weight_near + 1.0 + weight_far)


def shifted(block, left, right, coef_first, coef_last):
    size = block.shape[0]
    place = lax.broadcasted_iota(jnp.int32, (8, C), 0)
    before = pltpu.roll(block, 1, 0)
    after = pltpu.roll(block, size - 1, 0)
    before_parts, after_parts = [], []
    for n in range(size // COLS):
        first, middle, last = (slice(n * COLS + at, n * COLS + at + 8) for at in (0, 8, 16))
        before_parts += [
            jnp.where(place == 0, left[n], before[first]),
            before[middle],
            before[last] * coef_first,
        ]
        after_parts += [
            after[first] * coef_last,
            after[middle],
            jnp.where(place == 7, right[n], after[last]),
        ]
    return jnp.concatenate(before_parts, axis=0), block, jnp.concatenate(after_parts, axis=0)


def expand(margins, core, gain, row_coefs, spare, ahead, stacked, columns):
    fill_row_coefs(margins, row_coefs)
    coef_first, coef_last = column_coefs(margins)
    half_gain = 0.5 * gain
    zeros = [jnp.zeros((1, C), jnp.float32)] * 4
    spare[...] = jnp.zeros_like(spare)

    def lanes(b, e):
        return slice((3 * b + e) * C, (3 * b + e + 1) * C)

    def put(f, k, b, e, values, scale):
        if scale:
            values = [
                p * row_coefs[b // 2, pl.ds(2 * k + n, 1), :] for n, p in enumerate(values)
            ]
        values = jnp.concatenate(values, axis=0).astype(jnp.bfloat16)
        stacked[f][pl.ds(pl.multiple_of(k * PAIR, 16), PAIR), lanes(b, e)] = values

    ahead[...] = jnp.zeros_like(ahead)

    def two_rows(step, _):
        block = ahead[...]
        after = jnp.minimum(step, ROWS // 2 - 1)
        blocks = [
            core[pl.ds(pl.multiple_of(f * CELLS + after * PAIR, 16), PAIR), :].astype(jnp.float32)
            for f in range(2)
        ]
        if columns is not None:
            for f in range(2):
                for n in range(2):
                    first, last = n * COLS, n * COLS + COLS - 1
                    columns[0, f, pl.ds(2 * after + n, 1), :] = blocks[f][first : first + 1]
                    columns[1, f, pl.ds(2 * after + n, 1), :] = blocks[f][last : last + 1]
        ahead[...] = activated(jnp.concatenate(blocks, axis=0), half_gain)
        k = jnp.maximum(step - 1, 0)
        views = shifted(block, zeros, zeros, coef_first, coef_last)
        for f in range(2):
            for e in range(3):
                rows = [views[e][(2 * f + n) * COLS : (2 * f + n + 1) * COLS] for n in range(2)]
                put(f, k, 1, e, rows, False)
                odd = [spare[f, e], rows[0]]
                spare[f, e] = rows[1]
                put(f, k, 0, e, odd, True)
                put(f, jnp.maximum(k - 1, 0), 2, e, odd, True)
        return 0

    lax.fori_loop(0, ROWS // 2 + 1, two_rows, 0)
    for f in range(2):
        for e in range(3):
            put(f, ROWS // 2 - 1, 2, e, [spare[f, e], jnp.zeros((COLS, C), jnp.float32)], False)


def across(coef):
    return jnp.concatenate([coef] * (C // 128), axis=1)


def fill_row_coefs(margins, row_coefs):
    row = lax.broadcasted_iota(jnp.int32, (ROWS, 128), 0)
    for n, b in enumerate((0, 2)):
        row_coefs[n] = across(blend_coef(row, b, ROWS, margins[0, 2], margins[0, 3]))


def column_coefs(margins):
    place = lax.broadcasted_iota(jnp.int32, (8, 128), 0)
    coef_first = blend_coef(place + (COLS - 8), 0, COLS, margins[0, 0], margins[0, 1])
    coef_last = blend_coef(place, 2, COLS, margins[0, 0], margins[0, 1])
    return across(coef_first), across(coef_last)


def dot(a, b):
    return jnp.dot(a, b, preferred_element_type=jnp.float32)


def weights_of(weights, times):
    return jnp.concatenate([weights[a] for a in times], axis=1)


def add_products(to, rows_of, weights_of):
    third = DEPTH // 3

    def part(n, _):
        rows = pl.ds(pl.multiple_of((n // 3) * 192, 16), 192)
        depth = pl.ds(pl.multiple_of((n % 3) * third, 128), third)
        to(rows, dot(rows_of(rows, depth), weights_of(depth)))
        return 0

    lax.fori_loop(0, 3 * (CELLS // 192), part, 0)


def expand_own_kernel(
    margins,
    core,
    gain,
    weights,
    early,
    own,
    columns,
    taps,
    row_coefs,
    spare,
    ahead,
    cells,
    late,
    sems,
):
    copies = [
        pltpu.make_async_copy(weights.at[2 - n], taps.at[:, pl.ds(n * C, C)], sems.at[n])
        for n in range(3)
    ]
    for copy in copies:
        copy.start()
    own[...] = jnp.zeros_like(own)
    expand(margins, core, gain[...].reshape(1, C), row_coefs, spare, ahead, (early, late), cells)
    columns[...] = cells[...].astype(jnp.bfloat16)
    copies[0].wait()

    def add(rows, product):
        own[rows, :] += product

    add_products(add, lambda rows, depth: late[rows, depth], lambda depth: taps[depth, :C])
    for copy in copies[1:]:
        copy.wait()


def own_kernel(early, taps, late, own):
    own[0] = jnp.zeros_like(late)
    own[1] = late[...]

    def add(rows, product):
        own[0, rows, :] += product[:, :C]
        own[1, rows, :] += product[:, C:]

    add_products(add, lambda rows, depth: early[rows, depth], lambda depth: taps[depth, : 2 * C])


def expand_previous_kernel(
    margins, group_slot, group, core, gain, stacked, row_coefs, spare, ahead
):
    gain = jnp.where(group_slot[group[0]] > 0, gain[...].reshape(1, C), 0.0)
    expand(margins, core, gain, row_coefs, spare, ahead, (stacked.at[0], stacked.at[1]), None)


def previous_kernel(stacked, taps, own, bias, sums):
    bias = bias[...].reshape(1, C)

    def part(n, _):
        rows = pl.ds(pl.multiple_of(n * 128, 16), 128)
        both = dot(stacked[1, rows, :], taps[:, C:])
        last = dot(stacked[0, rows, :], taps[:, 2 * C :])
        sums[0, rows, :] = own[0, rows, :] + bias + both[:, :C] + last
        sums[1, rows, :] = own[1, rows, :] + bias + both[:, C:]
        return 0

    lax.fori_loop(0, CELLS // 128, part, 0)


def join_kernel(
    margins,
    tile_row,
    group_slot,
    group,
    halo,
    halo_previous,
    gain,
    taps,
    sides,
    near,
    row_coefs,
    columns,
    rims,
):
    fill_row_coefs(margins, row_coefs)
    coef_first, coef_last = column_coefs(margins)
    half_gain = 0.5 * gain[...].reshape(1, C)
    half_previous = jnp.where(group_slot[group[0]] > 0, half_gain, 0.0)
    top = tile_row[0] == 1
    none = jnp.zeros((1, C), jnp.float32)

    def frames(f, _):
        for n, (source, scale) in enumerate(((halo_previous, half_previous), (halo, half_gain))):
            rim, left, right = (
                activated(source[part, f].astype(jnp.float32), scale) for part in range(3)
            )
            views = shifted(
                rim, [left[ROWS : ROWS + 1]], [right[ROWS : ROWS + 1]], coef_first, coef_last
            )
            at = 2 * n + f
            for e in range(3):
                values = jnp.concatenate([views[e], jnp.zeros((8, C), jnp.float32)], axis=0)
                rims[e, at * 32 : at * 32 + 32, :] = values.astype(jnp.bfloat16)
            for side, column in enumerate((left[:ROWS], right[:ROWS])):
                above = jnp.concatenate([none, column[: ROWS - 1]], axis=0) * row_coefs[0]
                below = jnp.concatenate([column[1:], none], axis=0) * row_coefs[1]
                for b, values in enumerate((above, column, below)):
                    rows = slice(at * ROWS, (at + 1) * ROWS)
                    columns[3 * side + b, rows, :] = values.astype(jnp.bfloat16)
        return 0

    for f in range(2):
        frames(f, 0)
    sides[...] = jnp.zeros_like(sides)
    near[...] = jnp.zeros_like(near)
    first = jnp.where(top, 0, 6)

    def times(a, _):
        lanes = pl.ds(pl.multiple_of((2 - a) * C, 128), C)

        def weight(row):
            return taps[pl.ds(pl.multiple_of(row * C, 16), C), lanes]

        rows = pl.ds(pl.multiple_of(a * ROWS, 16), 2 * ROWS)
        for side in range(2):
            sides[side] += sum(
                dot(columns[3 * side + b, rows, :], weight(3 * b + 2 * side)) for b in range(3)
            )
        rows = pl.ds(pl.multiple_of(a * 32, 32), 64)
        near[...] += sum(dot(rims[e, rows, :], weight(first + e)) for e in range(3))
        return 0

    lax.fori_loop(0, 3, times, 0)


def finish_kernel(tile_row, sums, sides, near, out):
    top = tile_row[0] == 1
    place = lax.broadcasted_iota(jnp.int32, (8, C), 0)
    for f in range(2):
        beside = near[32 * f : 32 * f + COLS]
        for k in range(ROWS // 2):
            block = sums[f, k * PAIR : (k + 1) * PAIR]
            parts = []
            for n in range(2):
                row = 2 * k + n
                values = block[n * COLS : (n + 1) * COLS]
                if row == 0:
                    values = values + jnp.where(top, beside, 0.0)
                if row == ROWS - 1:
                    values = values + jnp.where(top, 0.0, beside)
                at = slice(f * ROWS + row, f * ROWS + row + 1)
                parts += [
                    values[:8] + jnp.where(place == 0, sides[0, at], 0.0),
                    values[8:16],
                    values[16:] + jnp.where(place == 7, sides[1, at], 0.0),
                ]
            rows = slice(f * CELLS + k * PAIR, f * CELLS + (k + 1) * PAIR)
            out[rows] = jnp.concatenate(parts, axis=0).astype(jnp.bfloat16)


SMEM, VMEM, HBM = (pl.BlockSpec(memory_space=m) for m in (pltpu.SMEM, pltpu.VMEM, pl.ANY))
COEFS = pltpu.VMEM((2, ROWS, C), jnp.float32)
SPARE = pltpu.VMEM((2, 3, COLS, C), jnp.float32)
AHEAD = pltpu.VMEM((2 * PAIR, C), jnp.float32)
PARTIAL = jax.ShapeDtypeStruct((2, CELLS, C), jnp.float32)


def call(kernel, inputs, specs, outputs, scratch, flops, mib):
    many = isinstance(outputs, list)
    return pl.pallas_call(
        kernel,
        in_specs=specs,
        out_specs=[VMEM] * len(outputs) if many else VMEM,
        out_shape=outputs,
        scratch_shapes=scratch,
        compiler_params=pltpu.CompilerParams(vmem_limit_bytes=mib * 2**20),
        cost_estimate=pl.CostEstimate(
            flops=flops, bytes_accessed=flops // 2**10, transcendentals=0
        ),
    )(*inputs)


def prepare_kernel(core, group_slot, tile_row, index, rim, slots, sems):
    row = jnp.where(tile_row[0] == 1, 0, ROWS - 1)
    copies = [pltpu.make_async_copy(group_slot, slots, sems.at[2])] + [
        pltpu.make_async_copy(core.at[0, f, row], rim.at[f], sems.at[f]) for f in range(2)
    ]
    for copy in copies:
        copy.start()
    copies[0].wait()
    away = [(slots[d] - slots[0] + 4) % 4 for d in (1, 2, 3)]
    index[0] = (away[0] - 1) * 2 + jnp.where(away[1] > away[2], 1, 0)
    for copy in copies[1:]:
        copy.wait()


def prepare(features, group_slot, tile_row):
    return pl.pallas_call(
        prepare_kernel,
        in_specs=[HBM, HBM, SMEM],
        out_specs=[SMEM, VMEM],
        out_shape=[
            jax.ShapeDtypeStruct((1,), jnp.int32),
            jax.ShapeDtypeStruct((2, COLS, C), jnp.bfloat16),
        ],
        scratch_shapes=[pltpu.SMEM((4,), jnp.int32), pltpu.SemaphoreType.DMA((3,))],
    )(features, group_slot, tile_row)


def cyclic_order(index):
    place = index // 2 + 1
    others = [p for p in (1, 2, 3) if p != place]
    if index % 2:
        others = others[::-1]
    places = [0, place] + others
    return sorted(range(4), key=lambda d: places[d])


def local(features, group_slot, margins, norm_gain, kernel, conv_bias):
    tiles = lax.axis_size("tile")
    across = tiles // GRID_R
    tile_row = (lax.axis_index("tile") // across).astype(jnp.int32).reshape(1)
    group = lax.axis_index("group").astype(jnp.int32).reshape(1)
    weights = kernel.reshape(3, DEPTH, C)
    index, edge = prepare(features, group_slot, tile_row)
    conv_flops = 2 * 3 * CELLS * DEPTH * C

    def routed(order):
        route = [(order[n], order[(n + 1) % 4]) for n in range(4)]

        def branch(features, edge, margins, tile_row, group_slot, group, gain, weights, bias):
            previous = lax.ppermute(features, "group", route)
            rim = lax.ppermute(edge, "tile", [(t, (t + across) % tiles) for t in range(tiles)])
            early, late, columns, taps = call(
                expand_own_kernel,
                (margins, features.reshape(2 * CELLS, C), gain, weights),
                [SMEM, VMEM, VMEM, HBM],
                [
                    jax.ShapeDtypeStruct((CELLS, DEPTH), jnp.bfloat16),
                    jax.ShapeDtypeStruct((CELLS, C), jnp.float32),
                    jax.ShapeDtypeStruct((2, 2, ROWS, C), jnp.bfloat16),
                    jax.ShapeDtypeStruct((DEPTH, 3 * C), jnp.bfloat16),
                ],
                [
                    COEFS,
                    SPARE,
                    AHEAD,
                    pltpu.VMEM((2, 2, ROWS, C), jnp.float32),
                    pltpu.VMEM((CELLS, DEPTH), jnp.bfloat16),
                    pltpu.SemaphoreType.DMA((3,)),
                ],
                conv_flops // 3,
                8,
            )
            spare = jnp.zeros((2, COLS - ROWS - 1, C), jnp.bfloat16)
            first, last = (
                jnp.concatenate([columns[side], rim[:, at : at + 1], spare], axis=1)
                for side, at in ((0, 0), (1, COLS - 1))
            )
            inner = [t for t in range(tiles) if t % across != across - 1]
            left = lax.ppermute(last, "tile", [(t, t + 1) for t in inner])
            right = lax.ppermute(first, "tile", [(t + 1, t) for t in inner])
            own = call(
                own_kernel, (early, taps, late), [VMEM] * 3, PARTIAL, [], CELLS, 8
            )
            stacked = call(
                expand_previous_kernel,
                (margins, group_slot, group, previous.reshape(2 * CELLS, C), gain),
                [SMEM, SMEM, SMEM, VMEM, VMEM],
                jax.ShapeDtypeStruct((2, CELLS, DEPTH), jnp.bfloat16),
                [COEFS, SPARE, AHEAD],
                conv_flops // 3,
                8,
            )
            halo = jnp.stack([rim, left, right])
            halo, own = lax.optimization_barrier((halo, own))
            halo_previous = lax.ppermute(halo, "group", route)
            sums = call(
                previous_kernel, (stacked, taps, own, bias), [VMEM] * 4, PARTIAL, [], conv_flops, 8
            )
            halo_previous, sums = lax.optimization_barrier((halo_previous, sums))
            sides, near = call(
                join_kernel,
                (margins, tile_row, group_slot, group, halo, halo_previous, gain, taps),
                [SMEM] * 4 + [VMEM] * 4,
                [
                    jax.ShapeDtypeStruct((2, 2 * ROWS, C), jnp.float32),
                    jax.ShapeDtypeStruct((64, C), jnp.float32),
                ],
                [
                    COEFS,
                    pltpu.VMEM((6, 4 * ROWS, C), jnp.bfloat16),
                    pltpu.VMEM((3, 4 * 32, C), jnp.bfloat16),
                ],
                2 * 3 * 9 * 40 * C * C,
                8,
            )
            return sums, sides, near

        return branch

    sums, sides, near = lax.switch(
        index[0],
        [routed(cyclic_order(n)) for n in range(6)],
        features,
        edge,
        margins,
        tile_row,
        group_slot,
        group,
        norm_gain,
        weights,
        conv_bias,
    )
    decoded = call(
        finish_kernel,
        (tile_row, sums, sides, near),
        [SMEM, VMEM, VMEM, VMEM],
        jax.ShapeDtypeStruct((2 * CELLS, C), jnp.bfloat16),
        [],
        2 * CELLS * C,
        8,
    )
    return decoded.reshape(1, 2, ROWS, COLS, C)


def solution(mesh):
    return jax.shard_map(
        local,
        mesh=mesh,
        in_specs=(
            P(("video", "tile"), "group", None, None, None),
            P(),
            P("tile", None),
            P(),
            P(),
            P(),
        ),
        out_specs=P(("video", "tile"), "group", None, None, None),
        check_vma=False,
    )
```

```python
import jax
import jax.numpy as jnp
from jax import lax
from jax.experimental import pallas as pl
from jax.experimental.pallas import tpu as pltpu
from jax.sharding import PartitionSpec as P

GRID_R = 2
ROWS, COLS, C = 16, 24, 384
CELLS = ROWS * COLS
PAIR = 2 * COLS
DEPTH = 9 * C


def activated(values, half_gain):
    inv_norm = lax.rsqrt(jnp.mean(values * values, axis=-1, keepdims=True) + 1e-06)
    half = values * inv_norm * half_gain
    silu = half + half * jnp.tanh(half)
    return silu.astype(jnp.bfloat16).astype(jnp.float32)


def blend_coef(position, tap, core, near, far):
    source = position + (tap - 1)
    near_f, far_f = near.astype(jnp.float32), far.astype(jnp.float32)
    weight_near = jnp.maximum(near - position, 0).astype(jnp.float32) / (near_f + 1.0)
    weight_far = jnp.maximum(far + 1 - core + position, 0).astype(jnp.float32) / (far_f + 1.0)
    kept = jnp.where(source < near, weight_near, 0.0)
    kept = kept + jnp.where(source >= core - far, weight_far, 0.0)
    kept = kept + jnp.where((source >= -near) & (source < core + far), 1.0, 0.0)
    return kept / (weight_near + 1.0 + weight_far)


def shifted(block, left, right, coef_first, coef_last):
    size = block.shape[0]
    place = lax.broadcasted_iota(jnp.int32, (8, C), 0)
    before = pltpu.roll(block, 1, 0)
    after = pltpu.roll(block, size - 1, 0)
    before_parts, after_parts = [], []
    for n in range(size // COLS):
        first, middle, last = (slice(n * COLS + at, n * COLS + at + 8) for at in (0, 8, 16))
        before_parts += [
            jnp.where(place == 0, left[n], before[first]),
            before[middle],
            before[last] * coef_first,
        ]
        after_parts += [
            after[first] * coef_last,
            after[middle],
            jnp.where(place == 7, right[n], after[last]),
        ]
    return jnp.concatenate(before_parts, axis=0), block, jnp.concatenate(after_parts, axis=0)


def expand(margins, core, gain, row_coefs, spare, ahead, stacked, columns):
    fill_row_coefs(margins, row_coefs)
    coef_first, coef_last = column_coefs(margins)
    half_gain = 0.5 * gain
    zeros = [jnp.zeros((1, C), jnp.float32)] * 4
    spare[...] = jnp.zeros_like(spare)

    def lanes(b, e):
        return slice((3 * b + e) * C, (3 * b + e + 1) * C)

    def put(f, k, b, e, values, scale):
        if scale:
            values = [
                p * row_coefs[b // 2, pl.ds(2 * k + n, 1), :] for n, p in enumerate(values)
            ]
        values = jnp.concatenate(values, axis=0).astype(jnp.bfloat16)
        stacked[f][pl.ds(pl.multiple_of(k * PAIR, 16), PAIR), lanes(b, e)] = values

    ahead[...] = jnp.zeros_like(ahead)

    def two_rows(step, _):
        block = ahead[...]
        after = jnp.minimum(step, ROWS // 2 - 1)
        blocks = [
            core[pl.ds(pl.multiple_of(f * CELLS + after * PAIR, 16), PAIR), :].astype(jnp.float32)
            for f in range(2)
        ]
        if columns is not None:
            for f in range(2):
                for n in range(2):
                    first, last = n * COLS, n * COLS + COLS - 1
                    columns[0, f, pl.ds(2 * after + n, 1), :] = blocks[f][first : first + 1]
                    columns[1, f, pl.ds(2 * after + n, 1), :] = blocks[f][last : last + 1]
        ahead[...] = activated(jnp.concatenate(blocks, axis=0), half_gain)
        k = jnp.maximum(step - 1, 0)
        views = shifted(block, zeros, zeros, coef_first, coef_last)
        for f in range(2):
            for e in range(3):
                rows = [views[e][(2 * f + n) * COLS : (2 * f + n + 1) * COLS] for n in range(2)]
                put(f, k, 1, e, rows, False)
                odd = [spare[f, e], rows[0]]
                spare[f, e] = rows[1]
                put(f, k, 0, e, odd, True)
                put(f, jnp.maximum(k - 1, 0), 2, e, odd, True)
        return 0

    lax.fori_loop(0, ROWS // 2 + 1, two_rows, 0)
    for f in range(2):
        for e in range(3):
            put(f, ROWS // 2 - 1, 2, e, [spare[f, e], jnp.zeros((COLS, C), jnp.float32)], False)


def across(coef):
    return jnp.concatenate([coef] * (C // 128), axis=1)


def fill_row_coefs(margins, row_coefs):
    row = lax.broadcasted_iota(jnp.int32, (ROWS, 128), 0)
    for n, b in enumerate((0, 2)):
        row_coefs[n] = across(blend_coef(row, b, ROWS, margins[0, 2], margins[0, 3]))


def column_coefs(margins):
    place = lax.broadcasted_iota(jnp.int32, (8, 128), 0)
    coef_first = blend_coef(place + (COLS - 8), 0, COLS, margins[0, 0], margins[0, 1])
    coef_last = blend_coef(place, 2, COLS, margins[0, 0], margins[0, 1])
    return across(coef_first), across(coef_last)


def dot(a, b):
    return jnp.dot(a, b, preferred_element_type=jnp.float32)


def weights_of(weights, times):
    return jnp.concatenate([weights[a] for a in times], axis=1)


def add_products(to, rows_of, weights_of):
    third = DEPTH // 3

    def part(n, _):
        rows = pl.ds(pl.multiple_of((n // 3) * 192, 16), 192)
        depth = pl.ds(pl.multiple_of((n % 3) * third, 128), third)
        to(rows, dot(rows_of(rows, depth), weights_of(depth)))
        return 0

    lax.fori_loop(0, 3 * (CELLS // 192), part, 0)


def expand_own_kernel(
    margins,
    core,
    gain,
    weights,
    early,
    own,
    columns,
    taps,
    row_coefs,
    spare,
    ahead,
    cells,
    late,
    sems,
):
    copies = [
        pltpu.make_async_copy(weights.at[2 - n], taps.at[:, pl.ds(n * C, C)], sems.at[n])
        for n in range(3)
    ]
    for copy in copies:
        copy.start()
    own[...] = jnp.zeros_like(own)
    expand(margins, core, gain[...].reshape(1, C), row_coefs, spare, ahead, (early, late), cells)
    columns[...] = cells[...].astype(jnp.bfloat16)
    copies[0].wait()

    def add(rows, product):
        own[rows, :] += product

    add_products(add, lambda rows, depth: late[rows, depth], lambda depth: taps[depth, :C])
    for copy in copies[1:]:
        copy.wait()


def own_kernel(early, taps, late, own):
    own[0] = jnp.zeros_like(late)
    own[1] = late[...]

    def add(rows, product):
        own[0, rows, :] += product[:, :C]
        own[1, rows, :] += product[:, C:]

    add_products(add, lambda rows, depth: early[rows, depth], lambda depth: taps[depth, : 2 * C])


def expand_previous_kernel(
    margins, group_slot, group, core, gain, stacked, row_coefs, spare, ahead
):
    gain = jnp.where(group_slot[group[0]] > 0, gain[...].reshape(1, C), 0.0)
    expand(margins, core, gain, row_coefs, spare, ahead, (stacked.at[0], stacked.at[1]), None)


def previous_kernel(stacked, taps, own, bias, sums):
    bias = bias[...].reshape(1, C)

    def part(n, _):
        rows = pl.ds(pl.multiple_of(n * 128, 16), 128)
        both = dot(stacked[1, rows, :], taps[:, C:])
        last = dot(stacked[0, rows, :], taps[:, 2 * C :])
        sums[0, rows, :] = own[0, rows, :] + bias + both[:, :C] + last
        sums[1, rows, :] = own[1, rows, :] + bias + both[:, C:]
        return 0

    lax.fori_loop(0, CELLS // 128, part, 0)


def join_kernel(
    margins,
    tile_row,
    group_slot,
    group,
    halo,
    halo_previous,
    gain,
    taps,
    sums,
    out,
    row_coefs,
    sides,
    near,
    columns,
    rims,
):
    fill_row_coefs(margins, row_coefs)
    coef_first, coef_last = column_coefs(margins)
    half_gain = 0.5 * gain[...].reshape(1, C)
    half_previous = jnp.where(group_slot[group[0]] > 0, half_gain, 0.0)
    top = tile_row[0] == 1
    none = jnp.zeros((1, C), jnp.float32)

    def frames(f, _):
        for n, (source, scale) in enumerate(((halo_previous, half_previous), (halo, half_gain))):
            rim, left, right = (
                activated(source[part, f].astype(jnp.float32), scale) for part in range(3)
            )
            views = shifted(
                rim, [left[ROWS : ROWS + 1]], [right[ROWS : ROWS + 1]], coef_first, coef_last
            )
            at = 2 * n + f
            for e in range(3):
                values = jnp.concatenate([views[e], jnp.zeros((8, C), jnp.float32)], axis=0)
                rims[e, pl.ds(pl.multiple_of(at * 32, 32), 32), :] = values.astype(jnp.bfloat16)
            for side, column in enumerate((left[:ROWS], right[:ROWS])):
                above = jnp.concatenate([none, column[: ROWS - 1]], axis=0) * row_coefs[0]
                below = jnp.concatenate([column[1:], none], axis=0) * row_coefs[1]
                for b, values in enumerate((above, column, below)):
                    rows = pl.ds(pl.multiple_of(at * ROWS, 16), ROWS)
                    columns[3 * side + b, rows, :] = values.astype(jnp.bfloat16)
        return 0

    lax.fori_loop(0, 2, frames, 0)
    sides[...] = jnp.zeros_like(sides)
    near[...] = jnp.zeros_like(near)
    first = jnp.where(top, 0, 6)

    def times(a, _):
        lanes = pl.ds(pl.multiple_of((2 - a) * C, 128), C)

        def weight(row):
            return taps[pl.ds(pl.multiple_of(row * C, 16), C), lanes]

        rows = pl.ds(pl.multiple_of(a * ROWS, 16), 2 * ROWS)
        for side in range(2):
            sides[side] += sum(
                dot(columns[3 * side + b, rows, :], weight(3 * b + 2 * side)) for b in range(3)
            )
        rows = pl.ds(pl.multiple_of(a * 32, 32), 64)
        near[...] += sum(dot(rims[e, rows, :], weight(first + e)) for e in range(3))
        return 0

    lax.fori_loop(0, 3, times, 0)
    place = lax.broadcasted_iota(jnp.int32, (8, C), 0)

    def two_rows(k, _):
        for f in range(2):
            block = sums[f, pl.ds(pl.multiple_of(k * PAIR, 16), PAIR), :]
            beside = near[32 * f : 32 * f + COLS]
            parts = []
            for n, here in enumerate((top & (k == 0), ~top & (k == ROWS // 2 - 1))):
                values = block[n * COLS : (n + 1) * COLS] + jnp.where(here, beside, 0.0)
                at = pl.ds(f * ROWS + 2 * k + n, 1)
                parts += [
                    values[:8] + jnp.where(place == 0, sides[0, at, :], 0.0),
                    values[8:16],
                    values[16:] + jnp.where(place == 7, sides[1, at, :], 0.0),
                ]
            rows = pl.ds(pl.multiple_of(f * CELLS + k * PAIR, 16), PAIR)
            out[rows, :] = jnp.concatenate(parts, axis=0).astype(jnp.bfloat16)
        return 0

    lax.fori_loop(0, ROWS // 2, two_rows, 0)


SMEM, VMEM, HBM = (pl.BlockSpec(memory_space=m) for m in (pltpu.SMEM, pltpu.VMEM, pl.ANY))
COEFS = pltpu.VMEM((2, ROWS, C), jnp.float32)
SPARE = pltpu.VMEM((2, 3, COLS, C), jnp.float32)
AHEAD = pltpu.VMEM((2 * PAIR, C), jnp.float32)
PARTIAL = jax.ShapeDtypeStruct((2, CELLS, C), jnp.float32)


def call(kernel, inputs, specs, outputs, scratch, flops, mib):
    many = isinstance(outputs, list)
    return pl.pallas_call(
        kernel,
        in_specs=specs,
        out_specs=[VMEM] * len(outputs) if many else VMEM,
        out_shape=outputs,
        scratch_shapes=scratch,
        compiler_params=pltpu.CompilerParams(vmem_limit_bytes=mib * 2**20),
        cost_estimate=pl.CostEstimate(
            flops=flops, bytes_accessed=flops // 2**10, transcendentals=0
        ),
    )(*inputs)


def prepare_kernel(core, group_slot, tile_row, index, rim, slots, sems):
    row = jnp.where(tile_row[0] == 1, 0, ROWS - 1)
    copies = [pltpu.make_async_copy(group_slot, slots, sems.at[2])] + [
        pltpu.make_async_copy(core.at[0, f, row], rim.at[f], sems.at[f]) for f in range(2)
    ]
    for copy in copies:
        copy.start()
    copies[0].wait()
    away = [(slots[d] - slots[0] + 4) % 4 for d in (1, 2, 3)]
    index[0] = (away[0] - 1) * 2 + jnp.where(away[1] > away[2], 1, 0)
    for copy in copies[1:]:
        copy.wait()


def prepare(features, group_slot, tile_row):
    return pl.pallas_call(
        prepare_kernel,
        in_specs=[HBM, HBM, SMEM],
        out_specs=[SMEM, VMEM],
        out_shape=[
            jax.ShapeDtypeStruct((1,), jnp.int32),
            jax.ShapeDtypeStruct((2, COLS, C), jnp.bfloat16),
        ],
        scratch_shapes=[pltpu.SMEM((4,), jnp.int32), pltpu.SemaphoreType.DMA((3,))],
    )(features, group_slot, tile_row)


def cyclic_order(index):
    place = index // 2 + 1
    others = [p for p in (1, 2, 3) if p != place]
    if index % 2:
        others = others[::-1]
    places = [0, place] + others
    return sorted(range(4), key=lambda d: places[d])


def local(features, group_slot, margins, norm_gain, kernel, conv_bias):
    tiles = lax.axis_size("tile")
    across = tiles // GRID_R
    tile_row = (lax.axis_index("tile") // across).astype(jnp.int32).reshape(1)
    group = lax.axis_index("group").astype(jnp.int32).reshape(1)
    weights = kernel.reshape(3, DEPTH, C)
    index, edge = prepare(features, group_slot, tile_row)
    conv_flops = 2 * 3 * CELLS * DEPTH * C

    def routed(order):
        route = [(order[n], order[(n + 1) % 4]) for n in range(4)]

        def branch(features, edge, margins, tile_row, group_slot, group, gain, weights, bias):
            previous = lax.ppermute(features, "group", route)
            rim = lax.ppermute(edge, "tile", [(t, (t + across) % tiles) for t in range(tiles)])
            early, late, columns, taps = call(
                expand_own_kernel,
                (margins, features.reshape(2 * CELLS, C), gain, weights),
                [SMEM, VMEM, VMEM, HBM],
                [
                    jax.ShapeDtypeStruct((CELLS, DEPTH), jnp.bfloat16),
                    jax.ShapeDtypeStruct((CELLS, C), jnp.float32),
                    jax.ShapeDtypeStruct((2, 2, ROWS, C), jnp.bfloat16),
                    jax.ShapeDtypeStruct((DEPTH, 3 * C), jnp.bfloat16),
                ],
                [
                    COEFS,
                    SPARE,
                    AHEAD,
                    pltpu.VMEM((2, 2, ROWS, C), jnp.float32),
                    pltpu.VMEM((CELLS, DEPTH), jnp.bfloat16),
                    pltpu.SemaphoreType.DMA((3,)),
                ],
                conv_flops // 3,
                8,
            )
            spare = jnp.zeros((2, COLS - ROWS - 1, C), jnp.bfloat16)
            first, last = (
                jnp.concatenate([columns[side], rim[:, at : at + 1], spare], axis=1)
                for side, at in ((0, 0), (1, COLS - 1))
            )
            inner = [t for t in range(tiles) if t % across != across - 1]
            left = lax.ppermute(last, "tile", [(t, t + 1) for t in inner])
            right = lax.ppermute(first, "tile", [(t + 1, t) for t in inner])
            own = call(
                own_kernel, (early, taps, late), [VMEM] * 3, PARTIAL, [], CELLS, 8
            )
            stacked = call(
                expand_previous_kernel,
                (margins, group_slot, group, previous.reshape(2 * CELLS, C), gain),
                [SMEM, SMEM, SMEM, VMEM, VMEM],
                jax.ShapeDtypeStruct((2, CELLS, DEPTH), jnp.bfloat16),
                [COEFS, SPARE, AHEAD],
                conv_flops // 3,
                8,
            )
            halo = jnp.stack([rim, left, right])
            halo_previous = lax.ppermute(halo, "group", route)
            sums = call(
                previous_kernel, (stacked, taps, own, bias), [VMEM] * 4, PARTIAL, [], conv_flops, 8
            )
            return call(
                join_kernel,
                (margins, tile_row, group_slot, group, halo, halo_previous, gain, taps, sums),
                [SMEM] * 4 + [VMEM] * 5,
                jax.ShapeDtypeStruct((2 * CELLS, C), jnp.bfloat16),
                [
                    COEFS,
                    pltpu.VMEM((2, 2 * ROWS, C), jnp.float32),
                    pltpu.VMEM((64, C), jnp.float32),
                    pltpu.VMEM((6, 4 * ROWS, C), jnp.bfloat16),
                    pltpu.VMEM((3, 4 * 32, C), jnp.bfloat16),
                ],
                2 * 3 * 9 * 40 * C * C,
                8,
            )

        return branch

    decoded = lax.switch(
        index[0],
        [routed(cyclic_order(n)) for n in range(6)],
        features,
        edge,
        margins,
        tile_row,
        group_slot,
        group,
        norm_gain,
        weights,
        conv_bias,
    )
    return decoded.reshape(1, 2, ROWS, COLS, C)


def solution(mesh):
    return jax.shard_map(
        local,
        mesh=mesh,
        in_specs=(
            P(("video", "tile"), "group", None, None, None),
            P(),
            P("tile", None),
            P(),
            P(),
            P(),
        ),
        out_specs=P(("video", "tile"), "group", None, None, None),
        check_vma=False,
    )
```
